32 devices in a mesh: tok: 8 (over z, y), head: 4 (over x, core).
Axes of the slice: x: 2, y: 2, z: 4, core: 2. Of those that a mesh axis runs over, the one named last changes fastest.
Arguments:
- guess: float32 [1024, 512], P('tok', 'head'), may hold values from -4 to 4
- drive: float32 [1024, 512], P('tok', 'head'), may hold values from -2 to 2
- decay: float32 [1024, 512], P('tok', 'head'), may hold values from 0 to 1
- mixing: float32 [512], P('head'), may hold values from 0.1 to 0.5
- init_state: float32 [512], P('head'), may hold values from -6 to 6
- skew_gen: float32 [4, 128, 128], P('head'), as said below
- w_up: bfloat16 [512, 4096], P(None, 'head'), may hold values from -0.25 to 0.25
- w_down: bfloat16 [512, 4096], P(None, 'head'), may hold values from -0.09375 to 0.09375
- cotangent: bfloat16 [1024, 512], P('tok', 'head'), may hold values from -6 to 6
Outputs:
- states: float32 [1024, 512], P('tok', 'head')
- mlp_out: bfloat16 [1024, 512], P('tok', 'head')
- state_grad: bfloat16 [1024, 512], P('tok', 'head')
- grad_up: float32 [512, 4096], P('tok', 'head')
- grad_down: float32 [512, 4096], P('tok', 'head')
The draws below stay inside these ranges and needn't reach their ends.
Inputs may be any that keep to these rules, and one draw needn't show every extreme that they name: `skew_gen`: each head's matrix is skew-symmetric.
All inputs are finite; a program needn't handle non-finite values.
Results may differ from the reference program's by a relative error of at most 0.017.
Values may be sent and summed in bfloat16 or wider, within the bound.
No kernel may reach another device: no remote copies, remote signals or barrier semaphores. Data moves between devices by JAX's collectives and lax.ppermute only.
A program may use at most 64 MiB of HBM per device.

```python
import math
import jax
import jax.numpy as jnp
from jax import lax

STATE = 128
FF = 4096
TOK_DEV = 128
HEADS = 4
D = 512
SEQUENCE_TOKENS = 1024


def head_classes(key):
    order = jax.random.permutation(jax.random.fold_in(key, 101), HEADS)
    return order >= HEADS // 2


def per_channel(values):
    return jnp.repeat(values, STATE, axis=-1)


def head_noise(key, shape):
    return jnp.clip(jax.random.normal(key, shape, jnp.float32), -5.0, 5.0)


def draw_guess(key, part):
    lasting = head_classes(key)
    key_scale, key_noise = jax.random.split(jax.random.fold_in(key, 303))
    quick_scale = jax.random.uniform(key_scale, (HEADS,), jnp.float32, 0.3, 0.7)
    scales = jnp.where(lasting, 0.2 / math.sqrt(SEQUENCE_TOKENS), quick_scale)
    return head_noise(key_noise, (SEQUENCE_TOKENS, D)) * per_channel(scales)[None, :]


def draw_drive(key, part):
    lasting = head_classes(key)
    key_noise = jax.random.fold_in(key, 404)
    scales = jnp.where(lasting, 1.5 / math.sqrt(SEQUENCE_TOKENS), 0.3)
    return head_noise(key_noise, (SEQUENCE_TOKENS, D)) * per_channel(scales)[None, :]


def draw_decay(key, part):
    lasting = head_classes(key)
    key_slow, random_seed_fast, key_group, key_rough, key_spots = jax.random.split(jax.random.fold_in(key, 202), 5)
    slow_rate = 1.0 / (SEQUENCE_TOKENS * jnp.exp(jax.random.uniform(key_slow, (HEADS,), jnp.float32, math.log(2.0), math.log(8.0))))
    rapid_fraction = jnp.exp(jax.random.uniform(random_seed_fast, (HEADS,), jnp.float32, math.log(0.005), math.log(0.03)))
    attention_decay_speed = jnp.where(lasting, slow_rate, rapid_fraction)
    group_factor = jax.random.uniform(key_group, (SEQUENCE_TOKENS // TOK_DEV, HEADS), jnp.float32, 0.5, 1.5)
    roughness = jax.random.uniform(key_rough, (SEQUENCE_TOKENS, D), jnp.float32, 0.5, 1.5)
    decay_speeds = jnp.repeat(per_channel(attention_decay_speed[None, :] * group_factor), TOK_DEV, axis=0) * roughness
    kept_entry_selector = jnp.exp(-decay_speeds)
    flagged_spots = jax.random.randint(key_spots, (3,), 0, SEQUENCE_TOKENS)
    symbol_locations = jnp.arange(SEQUENCE_TOKENS)[:, None]
    vocabulary_groupings = jnp.any(symbol_locations == flagged_spots[None, :], axis=1)
    return jnp.where(vocabulary_groupings[:, None], 0.6 * kept_entry_selector, kept_entry_selector)


def draw_skew_gen(key, part):
    raw_values = jax.random.normal(key, (HEADS, STATE, STATE), jnp.float32) * (0.5 / math.sqrt(STATE))
    return raw_values - jnp.swapaxes(raw_values, 1, 2)


def spiked(values, rng, source, target, shards_of, factor):
    owner, partner = [(jnp.arange(values.shape[axis_at]) // (values.shape[axis_at] // shards_of)).reshape([-1 if axis == axis_at else 1 for axis in range(values.ndim)]) for axis_at in (source, target)]
    chosen = jax.random.permutation(rng, shards_of)[partner]
    strong = (owner == chosen) | (owner == (partner + shards_of // 2) % shards_of)
    return jnp.where(strong, factor * values, values)


def steps_of(key, dims, cuts, least, largest):
    def one(dim, shards_of):
        steps = jax.random.uniform(jax.random.fold_in(jax.random.fold_in(key, 6), dim), (shards_of,), jnp.float32, least / len(cuts), largest / len(cuts))
        return jnp.repeat(jnp.exp(steps), dims[dim] // shards_of).reshape((-1,) + (1,) * (len(dims) - dim - 1))

    gain = one(*cuts[0])
    for cut in cuts[1:]:
        gain = gain * one(*cut)
    return gain


def centred(key, shape, spread, most, cuts=(), held_as=jnp.bfloat16):
    level = steps_of(key, shape, cuts, -0.22, 0.18) if cuts else 1.0
    result = jax.random.normal(key, shape, jnp.float32) * spread * level
    return jnp.minimum(jnp.maximum(result, -most), most).astype(held_as)


def heavy_noise(key, shape, scale, bound, pieces, heavy, kind=jnp.bfloat16):
    result = scale * jax.random.normal(key, shape, jnp.float32)
    if pieces:
        result = result * steps_of(key, shape, pieces, -0.22, 0.18)
    return jnp.clip(spiked(result, jax.random.fold_in(key, 3), *heavy), -bound, bound).astype(kind)


def setup_inputs(seed: int = 0) -> dict:
    splits = jax.random.split(jax.random.key(seed), 10)
    return {
        "guess": draw_guess(jax.random.fold_in(splits[9], 71), 0),
        "drive": draw_drive(jax.random.fold_in(splits[9], 71), 0),
        "decay": draw_decay(jax.random.fold_in(splits[9], 71), 0),
        "mixing": jnp.clip(0.1 + 0.4 * jax.random.uniform(splits[3], (D,), jnp.float32) ** steps_of(splits[3], (D,), ((0, 4),), -0.2, 0.2), 0.1, 0.5),
        "init_state": centred(splits[4], (D,), 1.0, 6.0, ((0, 4),), jnp.float32),
        "skew_gen": draw_skew_gen(jax.random.fold_in(splits[9], 71), 0),
        "w_up": centred(splits[6], (D, FF), D ** -0.5, 0.25, ((1, 4),)),
        "w_down": centred(splits[7], (D, FF), FF ** -0.5, 0.09375, ((1, 4),)),
        "cotangent": heavy_noise(splits[8], (SEQUENCE_TOKENS, D), 1.0, 6.0, ((0, 8), (1, 4)), (0, 1, 8, 2.0)),
    }


exact_precision = lax.Precision.HIGHEST

def cayley(antisymmetric_matrix):
    identity = jnp.eye(antisymmetric_matrix.shape[0], dtype=jnp.float32)
    raised = identity + antisymmetric_matrix
    shifted = identity - jnp.dot(antisymmetric_matrix, antisymmetric_matrix, precision=exact_precision)
    factor = jnp.linalg.cholesky(shifted)
    squared = jnp.dot(raised, raised, precision=exact_precision)
    return jax.scipy.linalg.cho_solve((factor, True), squared.T).T

def tangent_approximate(before, decay, mixing):
    bent_values = jnp.tanh(before)
    curvature = 1.0 - bent_values * bent_values
    gradient_inclines = (1.0 - mixing) * decay + mixing * curvature
    pushes = mixing * (bent_values - curvature * before)
    return (gradient_inclines, pushes)

def reference(guess, drive, decay, mixing, init_state, skew_gen, w_up, w_down, cotangent):
    rotations = jax.vmap(cayley)(skew_gen)
    tokens_all = guess.shape[0]
    before = jnp.concatenate([init_state[None, :], guess[:-1]], axis=0)
    gradient_inclines, pushes = tangent_approximate(before, decay, mixing[None, :])
    gradient_inclines = gradient_inclines.reshape(tokens_all, HEADS, STATE)
    pushes = pushes.reshape(tokens_all, HEADS, STATE)
    offsets = jnp.einsum('hij,thj->thi', rotations, pushes, precision=exact_precision)
    offsets = offsets + drive.reshape(tokens_all, HEADS, STATE)

    def advance(carried, inputs):
        slope_row, bias_vector_line = inputs
        following = jnp.einsum('hij,hj->hi', rotations, slope_row * carried, precision=exact_precision) + bias_vector_line
        return (following, following)
    final_state, states = lax.scan(advance, init_state.reshape(HEADS, STATE), (gradient_inclines, offsets))
    states = states.reshape(tokens_all, HEADS * STATE)
    features = states.astype(jnp.bfloat16)
    hidden_pre = jnp.dot(features.astype(jnp.float32), w_up.astype(jnp.float32), preferred_element_type=jnp.float32)
    logistic_gate = jax.nn.sigmoid(hidden_pre)
    hidden = (hidden_pre * logistic_gate).astype(jnp.bfloat16)
    mlp_out = lax.dot_general(hidden.astype(jnp.float32), w_down.astype(jnp.float32), (((1,), (1,)), ((), ())), preferred_element_type=jnp.float32).astype(jnp.bfloat16)
    hidden_grad = jnp.dot(cotangent.astype(jnp.float32), w_down.astype(jnp.float32), preferred_element_type=jnp.float32)
    pre_grad = (hidden_grad * logistic_gate * (1.0 + hidden_pre * (1.0 - logistic_gate))).astype(jnp.bfloat16)
    state_grad = lax.dot_general(pre_grad.astype(jnp.float32), w_up.astype(jnp.float32), (((1,), (1,)), ((), ())), preferred_element_type=jnp.float32).astype(jnp.bfloat16)
    grad_up = lax.dot_general(features.astype(jnp.float32), pre_grad.astype(jnp.float32), (((0,), (0,)), ((), ())), preferred_element_type=jnp.float32)
    grad_down = lax.dot_general(cotangent.astype(jnp.float32), hidden.astype(jnp.float32), (((0,), (0,)), ((), ())), preferred_element_type=jnp.float32)
    return (states, mlp_out, state_grad, grad_up, grad_down)
```

```python
import functools

import jax
import jax.numpy as jnp
from jax import lax
from jax.experimental import pallas as pl
from jax.experimental.pallas import tpu as pltpu
from jax.sharding import PartitionSpec as P

BLOCKS = 8
PAD = 16
MIB = 1 << 20
bf16, f32 = jnp.bfloat16, jnp.float32
exact_precision = lax.Precision.HIGHEST
VMEM = pl.BlockSpec(memory_space=pltpu.VMEM)


def dot(a, b, dims=((1,), (0,)), precision=None):
    return lax.dot_general(a, b, (dims, ((), ())), precision=precision, preferred_element_type=f32)


def halves(x):
    high = x.astype(bf16)
    return high, (x - high.astype(f32)).astype(bf16)


def beside(x):
    return jnp.concatenate(halves(x), axis=1)


def stationary(w):
    high, low = halves(w)
    top = jnp.concatenate([high, low], axis=1)
    bottom = jnp.concatenate([high, jnp.zeros_like(low)], axis=1)
    return jnp.concatenate([top, bottom], axis=0)


def times(x, wide):
    n = x.shape[1]
    both = dot(beside(x), wide)
    return both[:, :n] + both[:, n:]


def unit(n):
    return (
        lax.broadcasted_iota(jnp.int32, (n, n), 0) == lax.broadcasted_iota(jnp.int32, (n, n), 1)
    ).astype(f32)


def turned(skew):
    n = skew.shape[0]
    eye = unit(n)
    gram = eye - times(skew, stationary(skew))
    bound = jnp.max(jnp.sum(jnp.abs(gram), axis=0, keepdims=True))
    scale = 2.0 / (1.0 + bound)
    rest = eye - scale * gram

    def going(carried):
        return jnp.logical_and(carried[2] > 1e-4, carried[3] < 40)

    def lap(carried):
        power, inverse, size, count = carried
        both = times(jnp.concatenate([power, inverse], axis=0), stationary(power))
        return both[:n], inverse + both[n:], size * size, count + 1

    size = (bound - 1.0) / (bound + 1.0)
    _, inverse, _, _ = lax.while_loop(going, lap, (rest, eye, size, jnp.int32(0)))
    near = times(eye - skew, stationary(scale * inverse))
    miss = eye - dot(eye + skew, near, precision=exact_precision)
    near = near + times(near, stationary(miss))
    return 2.0 * near - eye


def local_maps(skew, guess, halo, decay, drive, mixing, init, cot, message, starts, shifts, slopes, offsets, wide):
    rows, n = guess.shape
    steps = rows // BLOCKS
    rotation = turned(skew[...])
    wide_now = stationary(rotation)
    wide[...] = wide_now
    mix = mixing[...]
    first = jnp.where(lax.axis_index("tok") == 0, init[...], halo[...])
    row = lax.broadcasted_iota(jnp.int32, (rows, n), 0)
    before = jnp.where(row == 0, first, pltpu.roll(guess[...], 1, 0))
    bent = jnp.tanh(before)
    curve = 1.0 - bent * bent
    slopes[...] = (1.0 - mix) * decay[...] + mix * curve
    offsets[...] = times(mix * (bent - curve * before), wide_now) + drive[...]

    eye = unit(n)
    state = jnp.concatenate([eye] * BLOCKS + [jnp.zeros((BLOCKS, n), f32)], axis=0)
    for step in range(steps):
        slope = slopes[pl.ds(step, BLOCKS, stride=steps), :]
        spread = jnp.broadcast_to(slope[:, None, :], (BLOCKS, n, n)).reshape(BLOCKS * n, n)
        state = times(state * jnp.concatenate([spread, slope], axis=0), wide_now)
        shift = state[BLOCKS * n :] + offsets[pl.ds(step, BLOCKS, stride=steps), :]
        state = jnp.concatenate([state[: BLOCKS * n], shift], axis=0)
    shift = state[BLOCKS * n :]
    maps = [
        jnp.concatenate(
            [state[b * n : (b + 1) * n], jnp.broadcast_to(shift[b : b + 1], (8, n))], axis=0
        )
        for b in range(BLOCKS)
    ]
    tail = lax.broadcasted_iota(jnp.int32, (n + 8, n), 0) >= n
    reach = 1
    while reach < BLOCKS:
        joined = list(maps)
        for base in range(reach, BLOCKS, 2 * reach):
            for b in range(base, base + reach):
                moved = times(maps[base - 1], stationary(maps[b][:n]))
                last = jnp.broadcast_to(maps[b][n : n + 1], (n + 8, n))
                joined[b] = moved + jnp.where(tail, last, 0.0)
        maps = joined
        reach *= 2
    for b in range(BLOCKS - 1):
        starts[b * n : (b + 1) * n, :] = maps[b][:n].astype(bf16)
    shifts[0:1, :] = jnp.zeros((1, n), f32)
    for b in range(BLOCKS - 1):
        shifts[b + 1 : b + 2, :] = maps[b][n : n + 1]
    pack(message, maps[-1][:n], maps[-1][n : n + 1])
    message[n + PAD :, :] = cot[...]


def pack(message, whole, shift):
    n = whole.shape[1]
    message[:n, :] = whole.astype(bf16)
    high, low = halves(shift)
    line = lax.broadcasted_iota(jnp.int32, (PAD, n), 0)
    block = jnp.where(line == 0, high.astype(f32), jnp.where(line == 1, low.astype(f32), 0.0))
    message[n : n + PAD, :] = block.astype(bf16)


def unpack(block):
    n = block.shape[1]
    shift = block[n : n + PAD].astype(f32)
    return block[:n], shift[0:1] + shift[1:2]


def join_pair(mine, other, message):
    n = mine.shape[1]
    late = lax.rem(lax.axis_index("tok"), 2) == 1
    a, b = mine[: n + PAD, :], other[: n + PAD, :]
    early_map, early_shift = unpack(jnp.where(late, b, a))
    late_map, late_shift = unpack(jnp.where(late, a, b))
    whole = dot(early_map, late_map)
    doubled = jnp.concatenate([late_map, late_map], axis=0)
    shift = dot(jnp.broadcast_to(beside(early_shift), (PAD, 2 * n)), doubled)[0:1] + late_shift
    pack(message, whole, shift)
    rows = mine.shape[0] - n - PAD
    a, b = mine[n + PAD :, :], other[n + PAD :, :]
    message[n + PAD : n + PAD + rows, :] = jnp.where(late, b, a)
    message[n + PAD + rows :, :] = jnp.where(late, a, b)


def expand(near, pairs, init, starts, shifts, slopes, offsets, wide, states, features, cots, slots):
    rows, n = slopes.shape
    steps = rows // BLOCKS
    tok = lax.axis_index("tok")
    late, place = lax.rem(tok, 2) == 1, lax.div(tok, 2)
    head = n + PAD
    for k, pair in enumerate(pairs):
        at = jnp.bitwise_xor(place, k)
        slots[at] = pair[:head, :]
        cots[pl.ds(pl.multiple_of(at * 2 * rows, 2 * rows), 2 * rows), :] = pair[head:, :]

    def moved(current, block):
        whole, shift = unpack(block)
        return dot(beside(current), jnp.concatenate([whole, whole], axis=0)) + shift

    current = jnp.broadcast_to(init[...], (PAD, n))
    for q in range(len(pairs) - 1):
        current = jnp.where(q < place, moved(current, slots[q]), current)
    current = jnp.where(late, moved(current, near[:head, :]), current)
    split = beside(current)
    line = lax.broadcasted_iota(jnp.int32, (BLOCKS, n), 0)
    entry = jnp.where(line == 0, current[:BLOCKS], 0.0)
    for b in range(1, BLOCKS):
        start = starts[(b - 1) * n : b * n, :]
        got = dot(split, jnp.concatenate([start, start], axis=0))
        entry = jnp.where(line == b, got[:BLOCKS], entry)
    state = entry + shifts[...]
    wide_now = wide[...]
    for step in range(steps):
        picked = pl.ds(step, BLOCKS, stride=steps)
        state = times(state * slopes[picked, :], wide_now) + offsets[picked, :]
        states[picked, :] = state
    features[...] = states[...].astype(bf16)


def stack(pieces, out):
    rows = pieces[0].shape[0]
    place = lax.div(lax.axis_index("tok"), 2)
    for k, piece in enumerate(pieces):
        at = jnp.bitwise_xor(place, k)
        out[pl.ds(pl.multiple_of(at * rows, rows), rows), :] = piece[...]


def activate(pre, grad):
    gate = 1.0 / (1.0 + jnp.exp(-pre))
    hidden = (pre * gate).astype(bf16)
    return hidden, (grad * gate * (1.0 + pre * (1.0 - gate))).astype(bf16)


def own_tokens(heads, features, cots, w_up, w_down, all_features, all_cots, near_out, far_out):
    tok, head = lax.axis_index("tok"), lax.axis_index("head")
    n = cots[0].shape[1]
    places = lax.axis_size("tok") // 2
    rows = features[0].shape[0] // places
    half = lax.rem(tok, 2)
    for d in range(heads):
        column = pl.ds(pl.multiple_of(jnp.bitwise_xor(head, d) * n, n), n)
        all_cots[:, column] = cots[d][...]
        for side in range(2):
            piece = features[2 * d + side]
            for q in range(places):
                at = (2 * q + jnp.bitwise_xor(half, side)) * rows
                all_features[pl.ds(pl.multiple_of(at, rows), rows), column] = piece[
                    q * rows : (q + 1) * rows, :
                ]
    mine = pl.ds(pl.multiple_of(tok * rows, rows), rows)
    x, c = all_features[mine, :], all_cots[mine, :]
    hidden, pre_grad = activate(dot(x, w_up[...]), dot(c, w_down[...]))
    out = dot(hidden, w_down[...], ((1,), (1,)))
    back = dot(pre_grad, w_up[...], ((1,), (1,)))
    group = lax.div(head, 2)
    near_out[:rows, :] = jnp.zeros((rows, 2 * n), bf16)
    for x_at in range(heads // 2):
        columns = slice(2 * n * x_at, 2 * n * (x_at + 1))
        both = jnp.concatenate([out[:, columns], back[:, columns]], axis=0).astype(bf16)

        @pl.when(x_at == group)
        def _():
            near_out[...] = both

        for d in range(1, heads // 2):

            @pl.when(x_at == jnp.bitwise_xor(group, d))
            def _():
                far_out[d - 1][...] = both


def part_of(block, first, share):
    part = block[:share]
    for at in range(share, block.shape[0], share):
        part = jnp.where(first == at, block[at : at + share], part)
    return part


def gradients(features, cots, w_up, w_down, grad_up, grad_down):
    tok = lax.axis_index("tok")
    share = grad_up.shape[0]
    columns = w_up.shape[1]
    block = 128 if share < 128 else share
    base = lax.div(tok * share, block)
    inner = tok * share - base * block
    lanes = pl.ds(pl.multiple_of(base * block, block), block)
    x_side, c_side = features[:, lanes].T, cots[:, lanes].T
    chunk = 256

    def lap(i, _):
        at = pl.ds(pl.multiple_of(i * chunk, chunk), chunk)
        hidden, pre_grad = activate(dot(features[...], w_up[:, at]), dot(cots[...], w_down[:, at]))
        up, down = dot(x_side, pre_grad), dot(c_side, hidden)
        grad_up[:, at] = part_of(up, inner, share)
        grad_down[:, at] = part_of(down, inner, share)
        return 0

    lax.fori_loop(0, columns // chunk, lap, 0)


def fold(keep, arrived, near, away):
    n = near.shape[1]
    total = keep[...].astype(f32)
    for part in arrived:
        total = total + part[...].astype(f32)
    odd = lax.rem(lax.axis_index("head"), 2) == 1
    near[...] = jnp.where(odd, total[:, n:], total[:, :n])
    away[...] = jnp.where(odd, total[:, :n], total[:, n:]).astype(bf16)


def finish(near, arrived, out, back):
    rows = out.shape[0]
    total = near[...] + arrived[...].astype(f32)
    out[...] = total[:rows].astype(bf16)
    back[...] = total[rows:].astype(bf16)


def call(body, outs, *operands, scratch=(), limit=32 * MIB, flops=10**6, moved=10**5):
    return pl.pallas_call(
        body,
        out_shape=outs,
        in_specs=[VMEM] * len(operands),
        out_specs=jax.tree.map(lambda _: VMEM, outs),
        scratch_shapes=list(scratch),
        compiler_params=pltpu.CompilerParams(vmem_limit_bytes=limit),
        cost_estimate=pl.CostEstimate(flops=flops, bytes_accessed=moved, transcendentals=0),
    )(*operands)


def swap(block, tok_bits, head_bits):
    toks, heads = lax.axis_size("tok"), lax.axis_size("head")
    route = [
        (t * heads + h, (t ^ tok_bits) * heads + (h ^ head_bits))
        for t in range(toks)
        for h in range(heads)
    ]
    return lax.ppermute(block, ("tok", "head"), route)


def on_device(guess, drive, decay, mixing, init_state, skew_gen, w_up, w_down, cotangent):
    rows, n = guess.shape
    toks, heads = lax.axis_size("tok"), lax.axis_size("head")
    places = toks // 2
    S = jax.ShapeDtypeStruct
    init, mix = init_state[None, :], mixing[None, :]
    route = [(i, i + 1) for i in range(toks - 1)]
    halo = lax.ppermute(guess[rows - 1 :], "tok", route)

    message, starts, shifts, slopes, offsets, wide = call(
        local_maps,
        (
            S((n + PAD + rows, n), bf16),
            S(((BLOCKS - 1) * n, n), bf16),
            S((BLOCKS, n), f32),
            S((rows, n), f32),
            S((rows, n), f32),
            S((2 * n, 2 * n), bf16),
        ),
        skew_gen[0], guess, halo, decay, drive, mix, init, cotangent,
    )
    near = swap(message, 1, 0)
    pair = call(join_pair, S((n + PAD + 2 * rows, n), bf16), message, near)
    pairs = [pair] + [swap(pair, 2 * k, 0) for k in range(1, places)]

    def expand_all(*refs):
        count = len(pairs)
        expand(refs[0], refs[1 : 1 + count], *refs[1 + count :])

    states, features, cots = call(
        expand_all,
        (S((rows, n), f32), S((rows, n), bf16), S((toks * rows, n), bf16)),
        near, *pairs, init, starts, shifts, slopes, offsets, wide,
        scratch=[pltpu.VMEM((places, n + PAD, n), bf16)],
    )
    cot_parts = {0: cots}
    parts = [features] + [swap(features, 2 * k, 0) for k in range(1, places)]
    for d in range(2, heads, 2):
        cot_parts[d] = swap(cots, 0, d)
    lined = call(lambda *r: stack(r[:-1], r[-1]), S((places * rows, n), bf16), *parts)
    feature_parts = {(0, 0): lined}
    for d in range(0, heads, 2):
        for side in range(2):
            if (d, side) != (0, 0):
                feature_parts[d, side] = swap(lined, side, d)
    for d in range(0, heads, 2):
        cot_parts[d + 1] = swap(cot_parts[d], 0, 1)
        for side in range(2):
            feature_parts[d + 1, side] = swap(feature_parts[d, side], 0, 1)
    feature_list = [feature_parts[d, side] for d in range(heads) for side in range(2)]
    cot_list = [cot_parts[d] for d in range(heads)]
    tokens, width = toks * rows, heads * n
    hidden_units = w_up.shape[1]

    def own(*refs):
        f, refs = refs[: 2 * heads], refs[2 * heads :]
        c, refs = refs[:heads], refs[heads:]
        own_tokens(heads, f, c, *refs[:5], refs[5:])

    groups = heads // 2
    all_features, all_cots, keep, *far = call(
        own,
        (
            S((tokens, width), bf16),
            S((tokens, width), bf16),
            *[S((2 * rows, 2 * n), bf16) for _ in range(groups)],
        ),
        *feature_list, *cot_list, w_up, w_down, limit=56 * MIB,
    )
    arrived = [swap(far[d - 1], 0, 2 * d) for d in range(1, groups)]
    share = width // toks
    grad_up, grad_down = call(
        gradients,
        (S((share, hidden_units), f32), S((share, hidden_units), f32)),
        all_features, all_cots, w_up, w_down,
        limit=56 * MIB, flops=5 * 10**9, moved=4 * 10**6,
    )
    kept, away = call(
        lambda *r: fold(r[0], r[1:-2], *r[-2:]),
        (S((2 * rows, n), f32), S((2 * rows, n), bf16)),
        keep, *arrived,
    )
    mlp_out, state_grad = call(
        finish, (S((rows, n), bf16), S((rows, n), bf16)), kept, swap(away, 0, 1)
    )
    return (states, mlp_out, state_grad, grad_up, grad_down)


def solution(mesh):
    placed = (
        P("tok", "head"),
        P("tok", "head"),
        P("tok", "head"),
        P("head"),
        P("head"),
        P("head", None, None),
        P(None, "head"),
        P(None, "head"),
        P("tok", "head"),
    )
    return jax.shard_map(
        on_device,
        mesh=mesh,
        in_specs=placed,
        out_specs=(P("tok", "head"),) * 5,
        check_vma=False,
    )
```

```python
import functools

import jax
import jax.numpy as jnp
from jax import lax
from jax.experimental import pallas as pl
from jax.experimental.pallas import tpu as pltpu
from jax.sharding import PartitionSpec as P

BLOCKS = 8
PAD = 16
MIB = 1 << 20
bf16, f32 = jnp.bfloat16, jnp.float32
exact_precision = lax.Precision.HIGHEST
VMEM = pl.BlockSpec(memory_space=pltpu.VMEM)


def dot(a, b, dims=((1,), (0,)), precision=None):
    return lax.dot_general(a, b, (dims, ((), ())), precision=precision, preferred_element_type=f32)


def halves(x):
    high = x.astype(bf16)
    return high, (x - high.astype(f32)).astype(bf16)


def beside(x):
    return jnp.concatenate(halves(x), axis=1)


def stationary(w):
    high, low = halves(w)
    top = jnp.concatenate([high, low], axis=1)
    bottom = jnp.concatenate([high, jnp.zeros_like(low)], axis=1)
    return jnp.concatenate([top, bottom], axis=0)


def times(x, wide):
    n = x.shape[1]
    both = dot(beside(x), wide)
    return both[:, :n] + both[:, n:]


def unit(n):
    return (
        lax.broadcasted_iota(jnp.int32, (n, n), 0) == lax.broadcasted_iota(jnp.int32, (n, n), 1)
    ).astype(f32)


def turned(skew):
    n = skew.shape[0]
    eye = unit(n)
    gram = eye - times(skew, stationary(skew))
    bound = jnp.max(jnp.sum(jnp.abs(gram), axis=0, keepdims=True))
    scale = 2.0 / (1.0 + bound)
    rest = eye - scale * gram

    def going(carried):
        return jnp.logical_and(carried[2] > 1e-4, carried[3] < 40)

    def lap(carried):
        power, inverse, size, count = carried
        both = times(jnp.concatenate([power, inverse], axis=0), stationary(power))
        return both[:n], inverse + both[n:], size * size, count + 1

    size = (bound - 1.0) / (bound + 1.0)
    _, inverse, _, _ = lax.while_loop(going, lap, (rest, eye, size, jnp.int32(0)))
    near = times(eye - skew, stationary(scale * inverse))
    miss = eye - dot(eye + skew, near, precision=exact_precision)
    near = near + times(near, stationary(miss))
    return 2.0 * near - eye


def fetch(pairs, sems):
    copies = [pltpu.make_async_copy(a, b, sems.at[i]) for i, (a, b) in enumerate(pairs)]
    for copy in copies:
        copy.start()
    return copies


def cayley(skew, wide):
    wide[...] = stationary(turned(skew[0]))


def tangent(before, decay, mix):
    bent = jnp.tanh(before)
    curve = 1.0 - bent * bent
    return (1.0 - mix) * decay + mix * curve, mix * (bent - curve * before)


def local_maps(
    guess, decay, drive, mixing, init, wide, message, starts, shifts, slopes, offsets, lines
):
    rows, n = guess.shape
    steps = rows // BLOCKS
    wide_now = wide[...]
    slope, push = tangent(pltpu.roll(guess[...], 1, 0), decay[...], mixing[...])
    slopes[...] = slope
    offsets[...] = times(push, wide_now) + drive[...]
    own = [mixing[...], init[...], decay[0:1, :], drive[0:1, :]]
    lines[...] = jnp.concatenate(own + [jnp.zeros((4, n), f32)], axis=0)

    eye = unit(n)
    state = jnp.concatenate([eye] * BLOCKS + [jnp.zeros((BLOCKS, n), f32)], axis=0)
    line = lax.broadcasted_iota(jnp.int32, (BLOCKS, n), 0)
    for step in range(steps):
        slope = slopes[pl.ds(step, BLOCKS, stride=steps), :]
        spread = jnp.broadcast_to(slope[:, None, :], (BLOCKS, n, n)).reshape(BLOCKS * n, n)
        state = times(state * jnp.concatenate([spread, slope], axis=0), wide_now)
        shift = state[BLOCKS * n :] + offsets[pl.ds(step, BLOCKS, stride=steps), :]
        if step == 0:
            shift = jnp.where(line == 0, 0.0, shift)
            state = jnp.concatenate([eye, state[n : BLOCKS * n], shift], axis=0)
        else:
            state = jnp.concatenate([state[: BLOCKS * n], shift], axis=0)
    shift = state[BLOCKS * n :]
    maps = [
        jnp.concatenate(
            [state[b * n : (b + 1) * n], jnp.broadcast_to(shift[b : b + 1], (8, n))], axis=0
        )
        for b in range(BLOCKS)
    ]
    tail = lax.broadcasted_iota(jnp.int32, (n + 8, n), 0) >= n
    reach = 1
    while reach < BLOCKS:
        joined = list(maps)
        for base in range(reach, BLOCKS, 2 * reach):
            for b in range(base, base + reach):
                moved = times(maps[base - 1], stationary(maps[b][:n]))
                last = jnp.broadcast_to(maps[b][n : n + 1], (n + 8, n))
                joined[b] = moved + jnp.where(tail, last, 0.0)
        maps = joined
        reach *= 2
    shifts[0:1, :] = jnp.zeros((1, n), f32)
    for b in range(BLOCKS - 1):
        starts[b * n : (b + 1) * n, :] = maps[b][:n].astype(bf16)
        shifts[b + 1 : b + 2, :] = maps[b][n : n + 1]
    pack(message, maps[-1][:n], [maps[-1][n : n + 1], guess[rows - 1 :, :], decay[0:1, :], drive[0:1, :]])


def pack(message, whole, lines):
    n = whole.shape[1]
    message[:n, :] = whole.astype(bf16)
    parts = [part.astype(f32) for row in lines for part in halves(row)]
    parts.append(jnp.zeros((PAD - len(parts), n), f32))
    message[n : n + PAD, :] = jnp.concatenate(parts, axis=0).astype(bf16)


def unpack(block):
    n = block.shape[1]
    lines = block[n : n + PAD].astype(f32)
    return block[:n], [lines[2 * i : 2 * i + 1] + lines[2 * i + 1 : 2 * i + 2] for i in range(4)]


def doubled(whole):
    return jnp.concatenate([whole, whole], axis=0)


def join_pair(cot, mine, other, lines, wide, message, sems):
    n = mine.shape[1]
    copies = fetch([(cot, message.at[n + PAD :])], sems)
    late = lax.rem(lax.axis_index("tok"), 2) == 1
    a, b = mine[...], other[...]
    early_map, (early_shift, early_last, early_decay, early_drive) = unpack(jnp.where(late, b, a))
    late_map, (late_shift, late_last, late_decay, late_drive) = unpack(jnp.where(late, a, b))
    slope, push = tangent(early_last, late_decay, lines[0:1, :])
    first = jnp.broadcast_to(early_shift * slope + push, (8, n))
    crossed = times(jnp.concatenate([early_map.astype(f32) * slope, first], axis=0), wide[...])
    crossed = jnp.concatenate([crossed[:n], crossed[n:] + late_drive], axis=0)
    whole = dot(beside(crossed), doubled(late_map))
    pack(message, whole[:n], [whole[n : n + 1] + late_shift, late_last, early_decay, early_drive])
    copies[0].wait()


def expand(near, pairs, lines, starts, shifts, slopes, offsets, wide, states, features, cots, slots):
    rows, n = slopes.shape
    steps = rows // BLOCKS
    tok = lax.axis_index("tok")
    late, place = lax.rem(tok, 2) == 1, lax.div(tok, 2)
    head = n + PAD
    for k, pair in enumerate(pairs):
        at = jnp.bitwise_xor(place, k)
        slots[at] = pair[:head, :]
        cots[pl.ds(pl.multiple_of(at * rows, rows), rows), :] = pair[head:, :]
    mix, init, own_decay, own_drive = [lines[i : i + 1, :] for i in range(4)]
    wide_now = wide[...]

    def enter(current, last, decay, drive):
        slope, push = tangent(last, decay, mix)
        return times(current * slope + push, wide_now) + drive

    def passed(carried, block, taken):
        whole, (shift, last, decay, drive) = unpack(block)
        current = dot(beside(enter(*carried, decay, drive)), doubled(whole)) + shift
        return jnp.where(taken, current, carried[0]), jnp.where(taken, last, carried[1])

    carried = jnp.broadcast_to(init, (PAD, n)), init
    for q in range(len(pairs) - 1):
        carried = passed(carried, slots[q], q < place)
    carried = passed(carried, near[...], late)
    after = enter(*carried, own_decay, own_drive)
    split = beside(after)
    line = lax.broadcasted_iota(jnp.int32, (BLOCKS, n), 0)
    state = shifts[...]
    for b in range(1, BLOCKS):
        got = dot(split, doubled(starts[(b - 1) * n : b * n, :]))
        state = state + jnp.where(line == b, got[:BLOCKS], 0.0)
    for step in range(steps):
        picked = pl.ds(step, BLOCKS, stride=steps)
        state = times(state * slopes[picked, :], wide_now) + offsets[picked, :]
        if step == 0:
            state = jnp.where(line == 0, after[:BLOCKS], state)
        states[picked, :] = state
    features[...] = states[...].astype(bf16)


def stack(pieces, cots, lined, both):
    rows = pieces[0].shape[0]
    total = lined.shape[0]
    place = lax.div(lax.axis_index("tok"), 2)
    for k, piece in enumerate(pieces):
        at = pl.ds(pl.multiple_of(jnp.bitwise_xor(place, k) * rows, rows), rows)
        lined[at, :] = piece[...]
        both[at, :] = piece[...]
    both[total:, :] = cots[...]


def activate(pre, grad):
    gate = 0.5 + 0.5 * jnp.tanh(0.5 * pre)
    hidden = (pre * gate).astype(bf16)
    return hidden, (grad * gate * (1.0 + pre * (1.0 - gate))).astype(bf16)


def lay(pieces, place, out):
    head = lax.axis_index("head")
    rows = out.shape[0]
    for d, (piece, first) in enumerate(pieces):
        n = piece.shape[1]
        lanes = pl.ds(pl.multiple_of(jnp.bitwise_xor(head, d) * n, n), n)
        if place is None:
            out[:, lanes] = piece[first : first + rows, :]
        else:
            at = pl.multiple_of(first + place * rows, rows)
            out[:, lanes] = piece[pl.ds(at, rows), :]


def own_tokens(features, cots, w_up, w_down, outs, x, c):
    tok, head = lax.axis_index("tok"), lax.axis_index("head")
    n = features[0][0].shape[1]
    place = lax.div(tok, 2)
    lay(features, place, x)
    lay(cots, place, c)
    hidden, pre_grad = activate(dot(x[...], w_up[...]), dot(c[...], w_down[...]))
    out = dot(hidden, w_down[...], ((1,), (1,)))
    back = dot(pre_grad, w_up[...], ((1,), (1,)))
    group = lax.div(head, 2)
    groups = x.shape[1] // (2 * n)
    for at in range(groups):
        columns = slice(2 * n * at, 2 * n * (at + 1))
        both = jnp.concatenate([out[:, columns], back[:, columns]], axis=0).astype(bf16)
        for d in range(groups):

            @pl.when(jnp.bitwise_xor(group, d) == at)
            def _():
                outs[d][...] = both


def part_of(block, first, share):
    part = block[:share]
    for at in range(share, block.shape[0], share):
        part = jnp.where(first == at, block[at : at + share], part)
    return part


def gradients(features, cots, w_up, w_down, before, outs, x, c):
    tok = lax.axis_index("tok")
    share, columns = outs[0].shape
    lay(features, None, x)
    lay(cots, None, c)
    block = max(share, 128)
    base = lax.div(tok * share, block)
    inner = tok * share - base * block
    lanes = pl.ds(pl.multiple_of(base * block, block), block)
    x_side, c_side = x[:, lanes].T, c[:, lanes].T
    chunk = 256
    for first in range(0, columns, chunk):
        at = slice(first, first + chunk)
        hidden, pre_grad = activate(dot(x[...], w_up[:, at]), dot(c[...], w_down[:, at]))
        totals = dot(x_side, pre_grad), dot(c_side, hidden)
        for out, total, old in zip(outs, totals, before or (None, None)):
            total = part_of(total, inner, share)
            out[:, at] = total if old is None else total + old[:, at]


def fold(keep, arrived, near, away):
    n = near.shape[1]
    total = keep[...].astype(f32)
    for part in arrived:
        total = total + part[...].astype(f32)
    odd = lax.rem(lax.axis_index("head"), 2) == 1
    near[...] = jnp.where(odd, total[:, n:], total[:, :n])
    away[...] = jnp.where(odd, total[:, :n], total[:, n:]).astype(bf16)


def finish(near, arrived, out, back):
    rows = out.shape[0]
    total = near[...] + arrived[...].astype(f32)
    out[...] = total[:rows].astype(bf16)
    back[...] = total[rows:].astype(bf16)


def call(body, outs, *operands, far=(), scratch=(), limit=16 * MIB, flops=10**6, moved=10**5):
    held = [pl.BlockSpec(memory_space=pltpu.HBM) for _ in far]
    return pl.pallas_call(
        body,
        out_shape=outs,
        in_specs=held + [VMEM] * len(operands),
        out_specs=jax.tree.map(lambda _: VMEM, outs),
        scratch_shapes=list(scratch),
        compiler_params=pltpu.CompilerParams(vmem_limit_bytes=limit),
        cost_estimate=pl.CostEstimate(flops=flops, bytes_accessed=moved, transcendentals=0),
    )(*far, *operands)


def swap(block, tok_bits, head_bits):
    toks, heads = lax.axis_size("tok"), lax.axis_size("head")
    route = [
        (t * heads + h, (t ^ tok_bits) * heads + (h ^ head_bits))
        for t in range(toks)
        for h in range(heads)
    ]
    return lax.ppermute(block, ("tok", "head"), route)


def on_device(guess, drive, decay, mixing, init_state, skew_gen, w_up, w_down, cotangent):
    rows, n = guess.shape
    toks, heads = lax.axis_size("tok"), lax.axis_size("head")
    places = toks // 2
    S, dma = jax.ShapeDtypeStruct, pltpu.SemaphoreType.DMA
    init, mix = init_state[None, :], mixing[None, :]
    wide = call(cayley, S((2 * n, 2 * n), bf16), skew_gen, flops=3 * 10**9)
    message, starts, shifts, slopes, offsets, lines = call(
        local_maps,
        (
            S((n + PAD, n), bf16),
            S(((BLOCKS - 1) * n, n), bf16),
            S((BLOCKS, n), f32),
            S((rows, n), f32),
            S((rows, n), f32),
            S((8, n), f32),
        ),
        guess, decay, drive, mix, init, wide, flops=3 * 10**9,
    )
    near = swap(message, 1, 0)
    pair = call(
        join_pair, S((n + PAD + rows, n), bf16), message, near, lines, wide,
        far=(cotangent,), scratch=[dma((1,))],
    )
    pairs = [pair] + [swap(pair, 2 * k, 0) for k in range(1, places)]

    def expand_all(*refs):
        count = len(pairs)
        expand(refs[0], refs[1 : 1 + count], *refs[1 + count :])

    states, features, cots = call(
        expand_all,
        (S((rows, n), f32), S((rows, n), bf16), S((places * rows, n), bf16)),
        near, *pairs, lines, starts, shifts, slopes, offsets, wide,
        scratch=[pltpu.VMEM((places, n + PAD, n), bf16)], flops=3 * 10**9,
    )
    total = places * rows
    cot_x = {d: swap(cots, 0, d) for d in range(2, heads, 2)}
    parts = [features] + [swap(features, 2 * k, 0) for k in range(1, places)]
    lined, both = call(
        lambda *r: stack(r[:-3], *r[-3:]),
        (S((total, n), bf16), S((2 * total, n), bf16)),
        *parts, cots,
    )
    feature_x = {d: swap(lined, 0, d) for d in range(2, heads, 2)}
    side = {d: swap(both, 1, d) for d in range(0, heads, 2)}
    for d in range(0, heads, 2):
        if d:
            feature_x[d + 1] = swap(feature_x[d], 0, 1)
            cot_x[d + 1] = swap(cot_x[d], 0, 1)
        side[d + 1] = swap(side[d], 0, 1)
    core = swap(both, 0, 1)
    first_f = [both, core] + [feature_x[d] for d in range(2, heads)]
    first_c = [cot_x[d] for d in range(2, heads)]
    second = [side[d] for d in range(heads)]
    width = heads * n
    hidden_units = w_up.shape[1]
    limit = min(8 * MIB + 12 * total * width * 2, 56 * MIB)
    groups = heads // 2

    def parted(refs):
        f, c = refs[:heads], refs[heads : 2 * heads - 2]
        features = [(ref, 0) for ref in f]
        cots = [(ref, total) for ref in f[:2]] + [(ref, 0) for ref in c]
        return features, cots, refs[2 * heads - 2 :]

    def own(*refs):
        features, cots, refs = parted(refs)
        own_tokens(features, cots, refs[0], refs[1], refs[2 : 2 + groups], *refs[2 + groups :])

    keep, *far = call(
        own,
        tuple(S((2 * rows, 2 * n), bf16) for _ in range(groups)),
        *first_f, *first_c, w_up, w_down,
        scratch=[pltpu.VMEM((rows, width), bf16)] * 2, limit=limit,
        flops=10**9, moved=10**6,
    )
    arrived = [swap(far[d - 1], 0, 2 * d) for d in range(1, groups)]
    share = width // toks
    grads = (S((share, hidden_units), f32), S((share, hidden_units), f32))
    scratch = [pltpu.VMEM((total, width), bf16)] * 2

    def one(*refs):
        features, cots, refs = parted(refs)
        gradients(features, cots, refs[0], refs[1], None, refs[2:4], *refs[4:])

    half = call(
        one, grads, *first_f, *first_c, w_up, w_down,
        scratch=scratch, limit=limit, flops=3 * 10**9, moved=4 * 10**6,
    )

    def two(*refs):
        f, refs = refs[:heads], refs[heads:]
        features, cots = [(ref, 0) for ref in f], [(ref, total) for ref in f]
        gradients(features, cots, refs[0], refs[1], refs[2:4], refs[4:6], *refs[6:])

    grad_up, grad_down = call(
        two, grads, *second, w_up, w_down, *half,
        scratch=scratch, limit=limit, flops=3 * 10**9, moved=4 * 10**6,
    )
    kept, away = call(
        lambda *r: fold(r[1], r[2:-2], *r[-2:]),
        (S((2 * rows, n), f32), S((2 * rows, n), bf16)),
        half[0], keep, *arrived,
    )
    mlp_out, state_grad = call(
        finish, (S((rows, n), bf16), S((rows, n), bf16)), kept, swap(away, 0, 1)
    )
    return (states, mlp_out, state_grad, grad_up, grad_down)


def solution(mesh):
    placed = (
        P("tok", "head"),
        P("tok", "head"),
        P("tok", "head"),
        P("head"),
        P("head"),
        P("head", None, None),
        P(None, "head"),
        P(None, "head"),
        P("tok", "head"),
    )
    return jax.shard_map(
        on_device,
        mesh=mesh,
        in_specs=placed,
        out_specs=(P("tok", "head"),) * 5,
        check_vma=False,
    )
```

```python
import functools

import jax
import jax.numpy as jnp
from jax import lax
from jax.experimental import pallas as pl
from jax.experimental.pallas import tpu as pltpu
from jax.sharding import PartitionSpec as P

BLOCKS = 16
PAD = 16
MIB = 1 << 20
bf16, f32 = jnp.bfloat16, jnp.float32
exact_precision = lax.Precision.HIGHEST
VMEM = pl.BlockSpec(memory_space=pltpu.VMEM)


def dot(a, b, dims=((1,), (0,)), precision=None):
    return lax.dot_general(a, b, (dims, ((), ())), precision=precision, preferred_element_type=f32)


def halves(x):
    high = x.astype(bf16)
    return high, (x - high.astype(f32)).astype(bf16)


def beside(x):
    return jnp.concatenate(halves(x), axis=1)


def stationary(w):
    high, low = halves(w)
    top = jnp.concatenate([high, low], axis=1)
    bottom = jnp.concatenate([high, jnp.zeros_like(low)], axis=1)
    return jnp.concatenate([top, bottom], axis=0)


def times(x, wide):
    n = x.shape[1]
    both = dot(beside(x), wide)
    return both[:, :n] + both[:, n:]


def unit(n):
    return (
        lax.broadcasted_iota(jnp.int32, (n, n), 0) == lax.broadcasted_iota(jnp.int32, (n, n), 1)
    ).astype(f32)


def turned(skew):
    n = skew.shape[0]
    eye = unit(n)
    gram = eye - times(skew, stationary(skew))
    bound = jnp.max(jnp.sum(jnp.abs(gram), axis=0, keepdims=True))
    scale = 2.0 / (1.0 + bound)
    rest = eye - scale * gram

    def going(carried):
        return jnp.logical_and(carried[2] > 1e-4, carried[3] < 40)

    def lap(carried):
        power, inverse, size, count = carried
        both = times(jnp.concatenate([power, inverse], axis=0), stationary(power))
        return both[:n], inverse + both[n:], size * size, count + 1

    size = (bound - 1.0) / (bound + 1.0)
    _, inverse, _, _ = lax.while_loop(going, lap, (rest, eye, size, jnp.int32(0)))
    near = times(eye - skew, stationary(scale * inverse))
    miss = eye - dot(eye + skew, near, precision=exact_precision)
    near = near + times(near, stationary(miss))
    return 2.0 * near - eye


def fetch(pairs, sems):
    copies = [pltpu.make_async_copy(a, b, sems.at[i]) for i, (a, b) in enumerate(pairs)]
    for copy in copies:
        copy.start()
    return copies


def cayley(skew, wide):
    wide[...] = stationary(turned(skew[0]))


def tangent(before, decay, mix):
    bent = jnp.tanh(before)
    curve = 1.0 - bent * bent
    return (1.0 - mix) * decay + mix * curve, mix * (bent - curve * before)


def local_maps(
    guess, decay, drive, mixing, init, cot, wide,
    message, starts, shifts, slopes, offsets, lines, cot_out,
):
    rows, n = guess.shape
    steps = rows // BLOCKS
    cot_out[...] = cot[...]
    wide_now = wide[...]
    slope, push = tangent(pltpu.roll(guess[...], 1, 0), decay[...], mixing[...])
    slopes[...] = slope
    offsets[...] = times(push, wide_now) + drive[...]
    own = [mixing[...], init[...], decay[0:1, :], drive[0:1, :]]
    lines[...] = jnp.concatenate(own + [jnp.zeros((4, n), f32)], axis=0)

    eye = unit(n)
    turn = wide_now[:n, :n].astype(f32) + wide_now[:n, n:].astype(f32)
    state = jnp.concatenate([eye] * BLOCKS + [jnp.zeros((BLOCKS, n), f32)], axis=0)
    line = lax.broadcasted_iota(jnp.int32, (BLOCKS, n), 0)
    for step in range(steps):
        slope = slopes[pl.ds(step, BLOCKS, stride=steps), :]
        spread = jnp.broadcast_to(slope[:, None, :], (BLOCKS, n, n)).reshape(BLOCKS * n, n)
        state = times(state * jnp.concatenate([spread, slope], axis=0), wide_now)
        shift = state[BLOCKS * n :] + offsets[pl.ds(step, BLOCKS, stride=steps), :]
        if step == 0:
            shift = jnp.where(line == 0, drive[0:1, :], shift)
            state = jnp.concatenate([turn, state[n : BLOCKS * n], shift], axis=0)
        else:
            state = jnp.concatenate([state[: BLOCKS * n], shift], axis=0)
    shift = state[BLOCKS * n :]
    maps = [
        jnp.concatenate(
            [state[b * n : (b + 1) * n], jnp.broadcast_to(shift[b : b + 1], (8, n))], axis=0
        )
        for b in range(BLOCKS)
    ]
    tail = lax.broadcasted_iota(jnp.int32, (n + 8, n), 0) >= n
    reach = 1
    while reach < BLOCKS:
        joined = list(maps)
        for base in range(reach, BLOCKS, 2 * reach):
            for b in range(base, base + reach):
                moved = times(maps[base - 1], stationary(maps[b][:n]))
                last = jnp.broadcast_to(maps[b][n : n + 1], (n + 8, n))
                joined[b] = moved + jnp.where(tail, last, 0.0)
        maps = joined
        reach *= 2
    shifts[0:1, :] = jnp.zeros((1, n), f32)
    for b in range(BLOCKS - 1):
        starts[b * n : (b + 1) * n, :] = maps[b][:n].astype(bf16)
        shifts[b + 1 : b + 2, :] = maps[b][n : n + 1]
    pack(message, maps[-1][:n], [maps[-1][n : n + 1], guess[rows - 1 :, :], decay[0:1, :]])


def pack(message, whole, lines):
    n = whole.shape[1]
    message[:n, :] = whole.astype(bf16)
    parts = [part.astype(f32) for row in lines for part in halves(row)]
    parts.append(jnp.zeros((PAD - len(parts), n), f32))
    message[n : n + PAD, :] = jnp.concatenate(parts, axis=0).astype(bf16)


def unpack(block):
    n = block.shape[1]
    lines = block[n : n + PAD].astype(f32)
    return block[:n], [lines[2 * i : 2 * i + 1] + lines[2 * i + 1 : 2 * i + 2] for i in range(3)]


def doubled(whole):
    return jnp.concatenate([whole, whole], axis=0)


def join_pair(mine, other, cot, cot_near, lines, message, cot_pair):
    rows, n = cot.shape
    late = lax.rem(lax.axis_index("tok"), 2) == 1
    a, b = cot[...], cot_near[...]
    cot_pair[:rows, :] = jnp.where(late, b, a)
    cot_pair[rows:, :] = jnp.where(late, a, b)
    a, b = mine[...], other[...]
    early_map, (early_shift, early_last, early_decay) = unpack(jnp.where(late, b, a))
    late_map, (late_shift, late_last, late_decay) = unpack(jnp.where(late, a, b))
    slope, push = tangent(early_last, late_decay, lines[0:1, :])
    first = jnp.broadcast_to(early_shift * slope + push, (8, n))
    crossed = jnp.concatenate([early_map.astype(f32) * slope, first], axis=0)
    whole = dot(beside(crossed), doubled(late_map))
    pack(message, whole[:n], [whole[n : n + 1] + late_shift, late_last, early_decay])


def expand(near, pairs, lines, starts, shifts, slopes, offsets, wide, states, features, slots):
    rows, n = slopes.shape
    steps = rows // BLOCKS
    tok = lax.axis_index("tok")
    late, place = lax.rem(tok, 2) == 1, lax.div(tok, 2)
    for k, pair in enumerate(pairs):
        at = jnp.bitwise_xor(place, k)
        slots[at] = pair[...]
    mix, init, own_decay, own_drive = [lines[i : i + 1, :] for i in range(4)]
    wide_now = wide[...]

    def enter(current, last, decay):
        slope, push = tangent(last, decay, mix)
        return current * slope + push

    def passed(carried, block, taken):
        whole, (shift, last, decay) = unpack(block)
        current = dot(beside(enter(*carried, decay)), doubled(whole)) + shift
        return jnp.where(taken, current, carried[0]), jnp.where(taken, last, carried[1])

    carried = jnp.broadcast_to(init, (PAD, n)), init
    for q in range(len(pairs) - 1):
        carried = passed(carried, slots[q], q < place)
    carried = passed(carried, near[...], late)
    entering = enter(*carried, own_decay)
    split = beside(entering)
    line = lax.broadcasted_iota(jnp.int32, (BLOCKS, n), 0)
    state = shifts[...]
    for b in range(1, BLOCKS):
        got = dot(split, doubled(starts[(b - 1) * n : b * n, :]))
        state = state + jnp.where(line == b, got[:BLOCKS], 0.0)
    for step in range(steps):
        picked = pl.ds(step, BLOCKS, stride=steps)
        moving, offset = state * slopes[picked, :], offsets[picked, :]
        if step == 0:
            moving = jnp.where(line == 0, entering[:BLOCKS], moving)
            offset = jnp.where(line == 0, own_drive, offset)
        state = times(moving, wide_now) + offset
        states[picked, :] = state
    features[...] = states[...].astype(bf16)


def stack(pieces, outs):
    rows = pieces[0].shape[0]
    place = lax.div(lax.axis_index("tok"), 2)
    for k, piece in enumerate(pieces):
        at = pl.ds(pl.multiple_of(jnp.bitwise_xor(place, k) * rows, rows), rows)
        for out in outs:
            out[at, :] = piece[...]


def activate(pre, grad):
    gate = 0.5 + 0.5 * jnp.tanh(0.5 * pre)
    hidden = (pre * gate).astype(bf16)
    return hidden, (grad * gate * (1.0 + pre * (1.0 - gate))).astype(bf16)


def lay(pieces, rows, side, out):
    tok, head = lax.axis_index("tok"), lax.axis_index("head")
    half, place = lax.rem(tok, 2), lax.div(tok, 2)
    places = range(out.shape[0] // rows)
    for d, (piece, first) in enumerate(pieces):
        n = piece.shape[1]
        lanes = pl.ds(pl.multiple_of(jnp.bitwise_xor(head, d) * n, n), n)
        whole = first is None
        for q in places:
            at = q if len(places) > 1 else place
            if whole:
                at = pl.ds(pl.multiple_of((2 * at + jnp.bitwise_xor(half, side)) * rows, rows), rows)
            else:
                at = pl.ds(pl.multiple_of(first + at * rows, rows), rows)
            out[q * rows : (q + 1) * rows, lanes] = piece[at, :]


def own_tokens(features, cots, w_up, w_down, outs, x, c):
    head = lax.axis_index("head")
    rows, n = x.shape[0], features[0][0].shape[1]
    lay(features, rows, 0, x)
    lay(cots, rows, 0, c)
    hidden, pre_grad = activate(dot(x[...], w_up[...]), dot(c[...], w_down[...]))
    out = dot(hidden, w_down[...], ((1,), (1,)))
    back = dot(pre_grad, w_up[...], ((1,), (1,)))
    group = lax.div(head, 2)
    groups = x.shape[1] // (2 * n)
    for at in range(groups):
        columns = slice(2 * n * at, 2 * n * (at + 1))
        both = jnp.concatenate([out[:, columns], back[:, columns]], axis=0).astype(bf16)
        for d in range(groups):

            @pl.when(jnp.bitwise_xor(group, d) == at)
            def _():
                outs[d][...] = both


def part_of(block, first, share):
    part = block[:share]
    for at in range(share, block.shape[0], share):
        part = jnp.where(first == at, block[at : at + share], part)
    return part


def gradients(features, cots, rows, side, w_up, w_down, before, outs, x, c):
    tok = lax.axis_index("tok")
    share, columns = outs[0].shape
    lay(features, rows, side, x)
    lay(cots, rows, side, c)
    block = max(share, 128)
    base = lax.div(tok * share, block)
    inner = tok * share - base * block
    lanes = pl.ds(pl.multiple_of(base * block, block), block)
    x_side, c_side = x[:, lanes].T, c[:, lanes].T
    chunk = 256
    for first in range(0, columns, chunk):
        at = slice(first, first + chunk)
        hidden, pre_grad = activate(dot(x[...], w_up[:, at]), dot(c[...], w_down[:, at]))
        totals = dot(x_side, pre_grad), dot(c_side, hidden)
        for out, total, old in zip(outs, totals, before or (None, None)):
            total = part_of(total, inner, share)
            out[:, at] = total if old is None else total + old[:, at]


def fold(keep, arrived, near, away):
    n = near.shape[1]
    total = keep[...].astype(f32)
    for part in arrived:
        total = total + part[...].astype(f32)
    odd = lax.rem(lax.axis_index("head"), 2) == 1
    near[...] = jnp.where(odd, total[:, n:], total[:, :n])
    away[...] = jnp.where(odd, total[:, :n], total[:, n:]).astype(bf16)


def finish(near, arrived, out, back):
    rows = out.shape[0]
    total = near[...] + arrived[...].astype(f32)
    out[...] = total[:rows].astype(bf16)
    back[...] = total[rows:].astype(bf16)


def call(body, outs, *operands, far=(), scratch=(), limit=16 * MIB, flops=10**6, moved=10**5):
    held = [pl.BlockSpec(memory_space=pltpu.HBM) for _ in far]
    return pl.pallas_call(
        body,
        out_shape=outs,
        in_specs=held + [VMEM] * len(operands),
        out_specs=jax.tree.map(lambda _: VMEM, outs),
        scratch_shapes=list(scratch),
        compiler_params=pltpu.CompilerParams(vmem_limit_bytes=limit),
        cost_estimate=pl.CostEstimate(flops=flops, bytes_accessed=moved, transcendentals=0),
    )(*far, *operands)


def swap(block, tok_bits, head_bits):
    toks, heads = lax.axis_size("tok"), lax.axis_size("head")
    route = [
        (t * heads + h, (t ^ tok_bits) * heads + (h ^ head_bits))
        for t in range(toks)
        for h in range(heads)
    ]
    return lax.ppermute(block, ("tok", "head"), route)


def on_device(guess, drive, decay, mixing, init_state, skew_gen, w_up, w_down, cotangent):
    rows, n = guess.shape
    toks, heads = lax.axis_size("tok"), lax.axis_size("head")
    places = toks // 2
    S, dma = jax.ShapeDtypeStruct, pltpu.SemaphoreType.DMA
    init, mix = init_state[None, :], mixing[None, :]
    wide = call(cayley, S((2 * n, 2 * n), bf16), skew_gen, flops=3 * 10**9)
    message, starts, shifts, slopes, offsets, lines, cot = call(
        local_maps,
        (
            S((n + PAD, n), bf16),
            S(((BLOCKS - 1) * n, n), bf16),
            S((BLOCKS, n), f32),
            S((rows, n), f32),
            S((rows, n), f32),
            S((8, n), f32),
            S((rows, n), bf16),
        ),
        guess, decay, drive, mix, init, cotangent, wide, flops=3 * 10**9,
    )
    near = swap(message, 1, 0)
    cot_near = swap(cot, 1, 0)
    pair, cot = call(
        join_pair, (S((n + PAD, n), bf16), S((2 * rows, n), bf16)),
        message, near, cot, cot_near, lines,
    )
    pairs = [pair] + [swap(pair, 2 * k, 0) for k in range(1, places)]
    cot_parts = [cot] + [swap(cot, 2 * k, 0) for k in range(1, places)]

    def expand_all(*refs):
        count = len(pairs)
        expand(refs[0], refs[1 : 1 + count], *refs[1 + count :])

    states, features = call(
        expand_all,
        (S((rows, n), f32), S((rows, n), bf16)),
        near, *pairs, lines, starts, shifts, slopes, offsets, wide,
        scratch=[pltpu.VMEM((places, n + PAD, n), bf16)], flops=3 * 10**9,
    )
    total = places * rows
    cots = {
        0: call(
            lambda *r: stack(r[1:-1], r[-1:]), S((toks * rows, n), bf16), features, *cot_parts
        )
    }
    parts = [features] + [swap(features, 2 * k, 0) for k in range(1, places)]
    for d in range(2, heads, 2):
        cots[d] = swap(cots[0], 0, d)
    lined = {0: call(lambda *r: stack(r[:-1], r[-1:]), S((total, n), bf16), *parts)}
    for d in range(2, heads, 2):
        lined[d] = swap(lined[0], 0, d)
    sides = [swap(lined[0], 1, d) for d in range(0, heads, 2)]
    for d in range(0, heads, 2):
        lined[d + 1] = swap(lined[d], 0, 1)
        cots[d + 1] = swap(cots[d], 0, 1)
    lined = [lined[d] for d in range(heads)]
    cots = [cots[d] for d in range(heads)]
    width = heads * n
    hidden_units = w_up.shape[1]
    limit = min(8 * MIB + 12 * total * width * 2, 56 * MIB)
    groups = heads // 2

    def parted(refs):
        features, cots = refs[:heads], refs[heads : 2 * heads]
        return [(ref, 0) for ref in features], [(ref, None) for ref in cots], refs[2 * heads :]

    def own(*refs):
        features, cots, refs = parted(refs)
        own_tokens(features, cots, refs[0], refs[1], refs[2 : 2 + groups], *refs[2 + groups :])

    keep, *far = call(
        own,
        tuple(S((2 * rows, 2 * n), bf16) for _ in range(groups)),
        *lined, *cots, w_up, w_down,
        scratch=[pltpu.VMEM((rows, width), bf16)] * 2, limit=limit,
        flops=10**9, moved=10**6,
    )
    arrived = [swap(far[d - 1], 0, 2 * d) for d in range(1, groups)]
    share = width // toks
    grads = (S((share, hidden_units), f32), S((share, hidden_units), f32))
    scratch = [pltpu.VMEM((total, width), bf16)] * 2

    def one(*refs):
        features, cots, refs = parted(refs)
        gradients(features, cots, rows, 0, refs[0], refs[1], None, refs[3:5], *refs[5:])

    half = call(
        one, grads, *lined, *cots, w_up, w_down, keep,
        scratch=scratch, limit=limit, flops=3 * 10**9, moved=4 * 10**6,
    )

    def line_up(*refs):
        for i, ref in enumerate(refs[1:-1]):
            refs[-1][i * total : (i + 1) * total, :] = ref[...]

    near_sides = call(line_up, S((groups * total, n), bf16), half[0], *sides)
    core_sides = swap(near_sides, 0, 1)

    def two(*refs):
        features = [(refs[d % 2], (d // 2) * total) for d in range(heads)]
        cots, refs = [(ref, None) for ref in refs[2 : 2 + heads]], refs[2 + heads :]
        gradients(features, cots, rows, 1, refs[0], refs[1], refs[2:4], refs[4:6], *refs[6:])

    grad_up, grad_down = call(
        two, grads, near_sides, core_sides, *cots, w_up, w_down, *half,
        scratch=scratch, limit=limit, flops=3 * 10**9, moved=4 * 10**6,
    )
    kept, away = call(
        lambda *r: fold(r[1], r[2:-2], *r[-2:]),
        (S((2 * rows, n), f32), S((2 * rows, n), bf16)),
        half[0], keep, *arrived, flops=4 * 10**9,
    )
    mlp_out, state_grad = call(
        finish, (S((rows, n), bf16), S((rows, n), bf16)), kept, swap(away, 0, 1), flops=4 * 10**9
    )
    return (states, mlp_out, state_grad, grad_up, grad_down)


def solution(mesh):
    placed = (
        P("tok", "head"),
        P("tok", "head"),
        P("tok", "head"),
        P("head"),
        P("head"),
        P("head", None, None),
        P(None, "head"),
        P(None, "head"),
        P("tok", "head"),
    )
    return jax.shard_map(
        on_device,
        mesh=mesh,
        in_specs=placed,
        out_specs=(P("tok", "head"),) * 5,
        check_vma=False,
    )
```

```python
import functools

import jax
import jax.numpy as jnp
from jax import lax
from jax.experimental import pallas as pl
from jax.experimental.pallas import tpu as pltpu
from jax.sharding import PartitionSpec as P

BLOCKS = 16
PAD = 16
MIB = 1 << 20
bf16, f32 = jnp.bfloat16, jnp.float32
exact_precision = lax.Precision.HIGHEST
VMEM = pl.BlockSpec(memory_space=pltpu.VMEM)


def dot(a, b, dims=((1,), (0,)), precision=None):
    return lax.dot_general(a, b, (dims, ((), ())), precision=precision, preferred_element_type=f32)


def halves(x):
    high = x.astype(bf16)
    return high, (x - high.astype(f32)).astype(bf16)


def beside(x):
    return jnp.concatenate(halves(x), axis=1)


def stationary(w):
    high, low = halves(w)
    top = jnp.concatenate([high, low], axis=1)
    bottom = jnp.concatenate([high, jnp.zeros_like(low)], axis=1)
    return jnp.concatenate([top, bottom], axis=0)


def times(x, wide):
    n = x.shape[1]
    both = dot(beside(x), wide)
    return both[:, :n] + both[:, n:]


def unit(n):
    return (
        lax.broadcasted_iota(jnp.int32, (n, n), 0) == lax.broadcasted_iota(jnp.int32, (n, n), 1)
    ).astype(f32)


def turned(skew):
    n = skew.shape[0]
    eye = unit(n)
    gram = eye - times(skew, stationary(skew))
    bound = jnp.max(jnp.sum(jnp.abs(gram), axis=0, keepdims=True))
    scale = 2.0 / (1.0 + bound)
    rest = eye - scale * gram

    def going(carried):
        return jnp.logical_and(carried[2] > 1e-4, carried[3] < 40)

    def lap(carried):
        power, inverse, size, count = carried
        both = times(jnp.concatenate([power, inverse], axis=0), stationary(power))
        return both[:n], inverse + both[n:], size * size, count + 1

    size = (bound - 1.0) / (bound + 1.0)
    _, inverse, _, _ = lax.while_loop(going, lap, (rest, eye, size, jnp.int32(0)))
    near = times(eye - skew, stationary(scale * inverse))
    miss = eye - dot(eye + skew, near, precision=exact_precision)
    near = near + times(near, stationary(miss))
    return 2.0 * near - eye


def fetch(pairs, sems):
    copies = [pltpu.make_async_copy(a, b, sems.at[i]) for i, (a, b) in enumerate(pairs)]
    for copy in copies:
        copy.start()
    return copies


def cayley(skew, wide):
    wide[...] = stationary(turned(skew[0]))


def tangent(before, decay, mix):
    bent = jnp.tanh(before)
    curve = 1.0 - bent * bent
    return (1.0 - mix) * decay + mix * curve, mix * (bent - curve * before)


def local_maps(
    guess, decay, drive, mixing, init, cot, wide,
    message, starts, shifts, slopes, offsets, lines, cot_out,
):
    rows, n = guess.shape
    steps = rows // BLOCKS
    cot_out[...] = cot[...]
    wide_now = wide[...]
    slope, push = tangent(pltpu.roll(guess[...], 1, 0), decay[...], mixing[...])
    slopes[...] = slope
    offsets[...] = times(push, wide_now) + drive[...]
    own = [mixing[...], init[...], decay[0:1, :], drive[0:1, :]]
    lines[...] = jnp.concatenate(own + [jnp.zeros((4, n), f32)], axis=0)

    eye = unit(n)
    turn = wide_now[:n, :n].astype(f32) + wide_now[:n, n:].astype(f32)
    state = jnp.concatenate([eye] * BLOCKS + [jnp.zeros((BLOCKS, n), f32)], axis=0)
    line = lax.broadcasted_iota(jnp.int32, (BLOCKS, n), 0)
    for step in range(steps):
        slope = slopes[pl.ds(step, BLOCKS, stride=steps), :]
        spread = jnp.broadcast_to(slope[:, None, :], (BLOCKS, n, n)).reshape(BLOCKS * n, n)
        state = times(state * jnp.concatenate([spread, slope], axis=0), wide_now)
        shift = state[BLOCKS * n :] + offsets[pl.ds(step, BLOCKS, stride=steps), :]
        if step == 0:
            shift = jnp.where(line == 0, drive[0:1, :], shift)
            state = jnp.concatenate([turn, state[n : BLOCKS * n], shift], axis=0)
        else:
            state = jnp.concatenate([state[: BLOCKS * n], shift], axis=0)
    shift = state[BLOCKS * n :]
    maps = [
        jnp.concatenate(
            [state[b * n : (b + 1) * n], jnp.broadcast_to(shift[b : b + 1], (8, n))], axis=0
        )
        for b in range(BLOCKS)
    ]
    tail = lax.broadcasted_iota(jnp.int32, (n + 8, n), 0) >= n
    reach = 1
    while reach < BLOCKS:
        joined = list(maps)
        for base in range(reach, BLOCKS, 2 * reach):
            for b in range(base, base + reach):
                moved = times(maps[base - 1], stationary(maps[b][:n]))
                last = jnp.broadcast_to(maps[b][n : n + 1], (n + 8, n))
                joined[b] = moved + jnp.where(tail, last, 0.0)
        maps = joined
        reach *= 2
    shifts[0:1, :] = jnp.zeros((1, n), f32)
    for b in range(BLOCKS - 1):
        starts[b * n : (b + 1) * n, :] = maps[b][:n].astype(bf16)
        shifts[b + 1 : b + 2, :] = maps[b][n : n + 1]
    pack(message, maps[-1][:n], [maps[-1][n : n + 1], guess[rows - 1 :, :], decay[0:1, :]])


def pack(message, whole, lines):
    n = whole.shape[1]
    message[:n, :] = whole.astype(bf16)
    parts = [part.astype(f32) for row in lines for part in halves(row)]
    parts.append(jnp.zeros((PAD - len(parts), n), f32))
    message[n : n + PAD, :] = jnp.concatenate(parts, axis=0).astype(bf16)


def unpack(block):
    n = block.shape[1]
    lines = block[n : n + PAD].astype(f32)
    return block[:n], [lines[2 * i : 2 * i + 1] + lines[2 * i + 1 : 2 * i + 2] for i in range(3)]


def doubled(whole):
    return jnp.concatenate([whole, whole], axis=0)


def join_pair(mine, other, cot, cot_near, lines, message, cot_pair):
    rows, n = cot.shape
    late = lax.rem(lax.axis_index("tok"), 2) == 1
    a, b = cot[...], cot_near[...]
    cot_pair[:rows, :] = jnp.where(late, b, a)
    cot_pair[rows:, :] = jnp.where(late, a, b)
    a, b = mine[...], other[...]
    early_map, (early_shift, early_last, early_decay) = unpack(jnp.where(late, b, a))
    late_map, (late_shift, late_last, late_decay) = unpack(jnp.where(late, a, b))
    slope, push = tangent(early_last, late_decay, lines[0:1, :])
    first = jnp.broadcast_to(early_shift * slope + push, (8, n))
    crossed = jnp.concatenate([early_map.astype(f32) * slope, first], axis=0)
    whole = dot(beside(crossed), doubled(late_map))
    pack(message, whole[:n], [whole[n : n + 1] + late_shift, late_last, early_decay])


def expand(near, pairs, lines, starts, shifts, slopes, offsets, wide, states, features, slots):
    rows, n = slopes.shape
    steps = rows // BLOCKS
    tok = lax.axis_index("tok")
    late, place = lax.rem(tok, 2) == 1, lax.div(tok, 2)
    for k, pair in enumerate(pairs):
        at = jnp.bitwise_xor(place, k)
        slots[at] = pair[...]
    mix, init, own_decay, own_drive = [lines[i : i + 1, :] for i in range(4)]
    wide_now = wide[...]

    def enter(current, last, decay):
        slope, push = tangent(last, decay, mix)
        return current * slope + push

    def passed(carried, block, taken):
        whole, (shift, last, decay) = unpack(block)
        current = dot(beside(enter(*carried, decay)), doubled(whole)) + shift
        return jnp.where(taken, current, carried[0]), jnp.where(taken, last, carried[1])

    carried = jnp.broadcast_to(init, (PAD, n)), init
    for q in range(len(pairs) - 1):
        carried = passed(carried, slots[q], q < place)
    carried = passed(carried, near[...], late)
    entering = enter(*carried, own_decay)
    split = beside(entering)
    line = lax.broadcasted_iota(jnp.int32, (BLOCKS, n), 0)
    state = shifts[...]
    for b in range(1, BLOCKS):
        got = dot(split, doubled(starts[(b - 1) * n : b * n, :]))
        state = state + jnp.where(line == b, got[:BLOCKS], 0.0)
    for step in range(steps):
        picked = pl.ds(step, BLOCKS, stride=steps)
        moving, offset = state * slopes[picked, :], offsets[picked, :]
        if step == 0:
            moving = jnp.where(line == 0, entering[:BLOCKS], moving)
            offset = jnp.where(line == 0, own_drive, offset)
        state = times(moving, wide_now) + offset
        states[picked, :] = state
    features[...] = states[...].astype(bf16)


def stack(pieces, outs):
    rows = pieces[0].shape[0]
    place = lax.div(lax.axis_index("tok"), 2)
    for k, piece in enumerate(pieces):
        at = pl.ds(pl.multiple_of(jnp.bitwise_xor(place, k) * rows, rows), rows)
        for out in outs:
            out[at, :] = piece[...]


def activate(pre, grad):
    gate = 0.5 + 0.5 * jnp.tanh(0.5 * pre)
    hidden = (pre * gate).astype(bf16)
    return hidden, (grad * gate * (1.0 + pre * (1.0 - gate))).astype(bf16)


def lay(pieces, rows, side, out):
    tok, head = lax.axis_index("tok"), lax.axis_index("head")
    half, place = lax.rem(tok, 2), lax.div(tok, 2)
    places = range(out.shape[0] // rows)
    for d, (piece, first) in enumerate(pieces):
        n = piece.shape[1]
        lanes = pl.ds(pl.multiple_of(jnp.bitwise_xor(head, d) * n, n), n)
        whole = first is None
        for q in places:
            at = q if len(places) > 1 else place
            if whole:
                at = pl.ds(pl.multiple_of((2 * at + jnp.bitwise_xor(half, side)) * rows, rows), rows)
            else:
                at = pl.ds(pl.multiple_of(first + at * rows, rows), rows)
            out[q * rows : (q + 1) * rows, lanes] = piece[at, :]


def own_tokens(features, cots, w_up, w_down, outs, x, c):
    head = lax.axis_index("head")
    rows, n = x.shape[0], features[0][0].shape[1]
    lay(features, rows, 0, x)
    lay(cots, rows, 0, c)
    hidden, pre_grad = activate(dot(x[...], w_up[...]), dot(c[...], w_down[...]))
    out = dot(hidden, w_down[...], ((1,), (1,)))
    back = dot(pre_grad, w_up[...], ((1,), (1,)))
    group = lax.div(head, 2)
    groups = x.shape[1] // (2 * n)
    for at in range(groups):
        columns = slice(2 * n * at, 2 * n * (at + 1))
        both = jnp.concatenate([out[:, columns], back[:, columns]], axis=0).astype(bf16)
        for d in range(groups):

            @pl.when(jnp.bitwise_xor(group, d) == at)
            def _():
                outs[d][...] = both


def part_of(block, first, share):
    part = block[:share]
    for at in range(share, block.shape[0], share):
        part = jnp.where(first == at, block[at : at + share], part)
    return part


def gradients(features, cots, rows, side, w_up, w_down, before, outs, x, c):
    tok = lax.axis_index("tok")
    share, columns = outs[0].shape
    lay(features, rows, side, x)
    lay(cots, rows, side, c)
    block = max(share, 128)
    base = lax.div(tok * share, block)
    inner = tok * share - base * block
    lanes = pl.ds(pl.multiple_of(base * block, block), block)
    x_side, c_side = x[:, lanes].T, c[:, lanes].T
    chunk = 256

    def inner_products(first):
        at = slice(first, first + chunk)
        return dot(x[...], w_up[:, at]), dot(c[...], w_down[:, at])

    ahead = inner_products(0)
    for first in range(0, columns, chunk):
        now, at = ahead, slice(first, first + chunk)
        if first + chunk < columns:
            ahead = inner_products(first + chunk)
        hidden, pre_grad = activate(*now)
        totals = dot(x_side, pre_grad), dot(c_side, hidden)
        for out, total, old in zip(outs, totals, before or (None, None)):
            total = part_of(total, inner, share)
            out[:, at] = total if old is None else total + old[:, at]


def fold(keep, arrived, near, away):
    n = near.shape[1]
    total = keep[...].astype(f32)
    for part in arrived:
        total = total + part[...].astype(f32)
    odd = lax.rem(lax.axis_index("head"), 2) == 1
    near[...] = jnp.where(odd, total[:, n:], total[:, :n])
    away[...] = jnp.where(odd, total[:, :n], total[:, n:]).astype(bf16)


def finish(near, arrived, out, back):
    rows = out.shape[0]
    total = near[...] + arrived[...].astype(f32)
    out[...] = total[:rows].astype(bf16)
    back[...] = total[rows:].astype(bf16)


def call(body, outs, *operands, far=(), scratch=(), limit=16 * MIB, flops=10**6, moved=10**5):
    held = [pl.BlockSpec(memory_space=pltpu.HBM) for _ in far]
    return pl.pallas_call(
        body,
        out_shape=outs,
        in_specs=held + [VMEM] * len(operands),
        out_specs=jax.tree.map(lambda _: VMEM, outs),
        scratch_shapes=list(scratch),
        compiler_params=pltpu.CompilerParams(vmem_limit_bytes=limit),
        cost_estimate=pl.CostEstimate(flops=flops, bytes_accessed=moved, transcendentals=0),
    )(*far, *operands)


def swap(block, tok_bits, head_bits):
    toks, heads = lax.axis_size("tok"), lax.axis_size("head")
    route = [
        (t * heads + h, (t ^ tok_bits) * heads + (h ^ head_bits))
        for t in range(toks)
        for h in range(heads)
    ]
    return lax.ppermute(block, ("tok", "head"), route)


def on_device(guess, drive, decay, mixing, init_state, skew_gen, w_up, w_down, cotangent):
    rows, n = guess.shape
    toks, heads = lax.axis_size("tok"), lax.axis_size("head")
    places = toks // 2
    S, dma = jax.ShapeDtypeStruct, pltpu.SemaphoreType.DMA
    init, mix = init_state[None, :], mixing[None, :]
    wide = call(cayley, S((2 * n, 2 * n), bf16), skew_gen, flops=3 * 10**9)
    message, starts, shifts, slopes, offsets, lines, cot = call(
        local_maps,
        (
            S((n + PAD, n), bf16),
            S(((BLOCKS - 1) * n, n), bf16),
            S((BLOCKS, n), f32),
            S((rows, n), f32),
            S((rows, n), f32),
            S((8, n), f32),
            S((rows, n), bf16),
        ),
        guess, decay, drive, mix, init, cotangent, wide, flops=3 * 10**9,
    )
    near = swap(message, 1, 0)
    cot_near = swap(cot, 1, 0)
    pair, cot = call(
        join_pair, (S((n + PAD, n), bf16), S((2 * rows, n), bf16)),
        message, near, cot, cot_near, lines,
    )
    pairs = [pair] + [swap(pair, 2 * k, 0) for k in range(1, places)]
    cot_parts = [cot] + [swap(cot, 2 * k, 0) for k in range(1, places)]

    def expand_all(*refs):
        count = len(pairs)
        expand(refs[0], refs[1 : 1 + count], *refs[1 + count :])

    states, features = call(
        expand_all,
        (S((rows, n), f32), S((rows, n), bf16)),
        near, *pairs, lines, starts, shifts, slopes, offsets, wide,
        scratch=[pltpu.VMEM((places, n + PAD, n), bf16)], flops=3 * 10**9,
    )
    total = places * rows
    cots = {
        0: call(
            lambda *r: stack(r[1:-1], r[-1:]), S((toks * rows, n), bf16), features, *cot_parts
        )
    }
    parts = [features] + [swap(features, 2 * k, 0) for k in range(1, places)]
    for d in range(2, heads, 2):
        cots[d] = swap(cots[0], 0, d)
    lined = {0: call(lambda *r: stack(r[:-1], r[-1:]), S((total, n), bf16), *parts)}
    for d in range(2, heads, 2):
        lined[d] = swap(lined[0], 0, d)
    sides = [swap(lined[0], 1, d) for d in range(0, heads, 2)]
    for d in range(0, heads, 2):
        lined[d + 1] = swap(lined[d], 0, 1)
        cots[d + 1] = swap(cots[d], 0, 1)
    lined = [lined[d] for d in range(heads)]
    cots = [cots[d] for d in range(heads)]
    width = heads * n
    hidden_units = w_up.shape[1]
    limit = min(8 * MIB + 12 * total * width * 2, 56 * MIB)
    groups = heads // 2

    def parted(refs):
        features, cots = refs[:heads], refs[heads : 2 * heads]
        return [(ref, 0) for ref in features], [(ref, None) for ref in cots], refs[2 * heads :]

    def own(*refs):
        features, cots, refs = parted(refs)
        own_tokens(features, cots, refs[0], refs[1], refs[2 : 2 + groups], *refs[2 + groups :])

    keep, *far = call(
        own,
        tuple(S((2 * rows, 2 * n), bf16) for _ in range(groups)),
        *lined, *cots, w_up, w_down,
        scratch=[pltpu.VMEM((rows, width), bf16)] * 2, limit=limit,
        flops=10**9, moved=10**6,
    )
    arrived = [swap(far[d - 1], 0, 2 * d) for d in range(1, groups)]
    share = width // toks
    grads = (S((share, hidden_units), f32), S((share, hidden_units), f32))
    scratch = [pltpu.VMEM((total, width), bf16)] * 2

    def one(*refs):
        features, cots, refs = parted(refs)
        gradients(features, cots, rows, 0, refs[0], refs[1], None, refs[3:5], *refs[5:])

    half = call(
        one, grads, *lined, *cots, w_up, w_down, keep,
        scratch=scratch, limit=limit, flops=3 * 10**9, moved=4 * 10**6,
    )

    def line_up(*refs):
        for i, ref in enumerate(refs[1:-1]):
            refs[-1][i * total : (i + 1) * total, :] = ref[...]

    near_sides = call(line_up, S((groups * total, n), bf16), half[0], *sides)
    core_sides = swap(near_sides, 0, 1)

    def two(*refs):
        features = [(refs[d % 2], (d // 2) * total) for d in range(heads)]
        cots, refs = [(ref, None) for ref in refs[2 : 2 + heads]], refs[2 + heads :]
        gradients(features, cots, rows, 1, refs[0], refs[1], refs[2:4], refs[4:6], *refs[6:])

    grad_up, grad_down = call(
        two, grads, near_sides, core_sides, *cots, w_up, w_down, *half,
        scratch=scratch, limit=limit, flops=3 * 10**9, moved=4 * 10**6,
    )
    kept, away = call(
        lambda *r: fold(r[1], r[2:-2], *r[-2:]),
        (S((2 * rows, n), f32), S((2 * rows, n), bf16)),
        half[0], keep, *arrived, flops=4 * 10**9,
    )
    mlp_out, state_grad = call(
        finish, (S((rows, n), bf16), S((rows, n), bf16)), kept, swap(away, 0, 1), flops=4 * 10**9
    )
    return (states, mlp_out, state_grad, grad_up, grad_down)


def solution(mesh):
    placed = (
        P("tok", "head"),
        P("tok", "head"),
        P("tok", "head"),
        P("head"),
        P("head"),
        P("head", None, None),
        P(None, "head"),
        P(None, "head"),
        P("tok", "head"),
    )
    return jax.shard_map(
        on_device,
        mesh=mesh,
        in_specs=placed,
        out_specs=(P("tok", "head"),) * 5,
        check_vma=False,
    )
```

```python
import functools

import jax
import jax.numpy as jnp
from jax import lax
from jax.experimental import pallas as pl
from jax.experimental.pallas import tpu as pltpu
from jax.sharding import PartitionSpec as P

BLOCKS = 16
PAD = 16
MIB = 1 << 20
bf16, f32 = jnp.bfloat16, jnp.float32
exact_precision = lax.Precision.HIGHEST
VMEM = pl.BlockSpec(memory_space=pltpu.VMEM)


def dot(a, b, dims=((1,), (0,)), precision=None):
    return lax.dot_general(a, b, (dims, ((), ())), precision=precision, preferred_element_type=f32)


def halves(x):
    high = x.astype(bf16)
    return high, (x - high.astype(f32)).astype(bf16)


def beside(x):
    return jnp.concatenate(halves(x), axis=1)


def stationary(w):
    high, low = halves(w)
    top = jnp.concatenate([high, low], axis=1)
    bottom = jnp.concatenate([high, jnp.zeros_like(low)], axis=1)
    return jnp.concatenate([top, bottom], axis=0)


def times(x, wide):
    n = x.shape[1]
    both = dot(beside(x), wide)
    return both[:, :n] + both[:, n:]


def unit(n):
    return (
        lax.broadcasted_iota(jnp.int32, (n, n), 0) == lax.broadcasted_iota(jnp.int32, (n, n), 1)
    ).astype(f32)


def turned(skew):
    n = skew.shape[0]
    eye = unit(n)
    gram = eye - times(skew, stationary(skew))
    bound = jnp.max(jnp.sum(jnp.abs(gram), axis=0, keepdims=True))
    scale = 2.0 / (1.0 + bound)
    rest = eye - scale * gram

    def going(carried):
        return jnp.logical_and(carried[2] > 1e-4, carried[3] < 40)

    def lap(carried):
        power, inverse, size, count = carried
        both = times(jnp.concatenate([power, inverse], axis=0), stationary(power))
        return both[:n], inverse + both[n:], size * size, count + 1

    size = (bound - 1.0) / (bound + 1.0)
    _, inverse, _, _ = lax.while_loop(going, lap, (rest, eye, size, jnp.int32(0)))
    near = times(eye - skew, stationary(scale * inverse))
    miss = eye - dot(eye + skew, near, precision=exact_precision)
    near = near + times(near, stationary(miss))
    return 2.0 * near - eye


def fetch(pairs, sems):
    copies = [pltpu.make_async_copy(a, b, sems.at[i]) for i, (a, b) in enumerate(pairs)]
    for copy in copies:
        copy.start()
    return copies


def cayley(skew, wide):
    wide[...] = stationary(turned(skew[0]))


def tangent(before, decay, mix):
    bent = jnp.tanh(before)
    curve = 1.0 - bent * bent
    return (1.0 - mix) * decay + mix * curve, mix * (bent - curve * before)


def local_maps(
    guess, decay, drive, mixing, init, cot, wide,
    message, starts, shifts, slopes, offsets, lines,
):
    rows, n = guess.shape
    steps = rows // BLOCKS
    message[n + PAD :, :] = cot[...]
    wide_now = wide[...]
    slope, push = tangent(pltpu.roll(guess[...], 1, 0), decay[...], mixing[...])
    slopes[...] = slope
    offsets[...] = times(push, wide_now) + drive[...]
    own = [mixing[...], init[...], decay[0:1, :], drive[0:1, :]]
    lines[...] = jnp.concatenate(own + [jnp.zeros((4, n), f32)], axis=0)

    eye = unit(n)
    turn = wide_now[:n, :n].astype(f32) + wide_now[:n, n:].astype(f32)
    state = jnp.concatenate([eye] * BLOCKS + [jnp.zeros((BLOCKS, n), f32)], axis=0)
    line = lax.broadcasted_iota(jnp.int32, (BLOCKS, n), 0)
    for step in range(steps):
        slope = slopes[pl.ds(step, BLOCKS, stride=steps), :]
        spread = jnp.broadcast_to(slope[:, None, :], (BLOCKS, n, n)).reshape(BLOCKS * n, n)
        state = times(state * jnp.concatenate([spread, slope], axis=0), wide_now)
        shift = state[BLOCKS * n :] + offsets[pl.ds(step, BLOCKS, stride=steps), :]
        if step == 0:
            shift = jnp.where(line == 0, drive[0:1, :], shift)
            state = jnp.concatenate([turn, state[n : BLOCKS * n], shift], axis=0)
        else:
            state = jnp.concatenate([state[: BLOCKS * n], shift], axis=0)
    shift = state[BLOCKS * n :]
    maps = [
        jnp.concatenate(
            [state[b * n : (b + 1) * n], jnp.broadcast_to(shift[b : b + 1], (8, n))], axis=0
        )
        for b in range(BLOCKS)
    ]
    tail = lax.broadcasted_iota(jnp.int32, (n + 8, n), 0) >= n
    reach = 1
    while reach < BLOCKS:
        joined = list(maps)
        for base in range(reach, BLOCKS, 2 * reach):
            for b in range(base, base + reach):
                moved = times(maps[base - 1], stationary(maps[b][:n]))
                last = jnp.broadcast_to(maps[b][n : n + 1], (n + 8, n))
                joined[b] = moved + jnp.where(tail, last, 0.0)
        maps = joined
        reach *= 2
    shifts[0:1, :] = jnp.zeros((1, n), f32)
    for b in range(BLOCKS - 1):
        starts[b * n : (b + 1) * n, :] = maps[b][:n].astype(bf16)
        shifts[b + 1 : b + 2, :] = maps[b][n : n + 1]
    pack(message, maps[-1][:n], [maps[-1][n : n + 1], guess[rows - 1 :, :], decay[0:1, :]])


def pack(message, whole, lines):
    n = whole.shape[1]
    message[:n, :] = whole.astype(bf16)
    parts = [part.astype(f32) for row in lines for part in halves(row)]
    parts.append(jnp.zeros((PAD - len(parts), n), f32))
    message[n : n + PAD, :] = jnp.concatenate(parts, axis=0).astype(bf16)


def unpack(block):
    n = block.shape[1]
    lines = block[n : n + PAD].astype(f32)
    return block[:n], [lines[2 * i : 2 * i + 1] + lines[2 * i + 1 : 2 * i + 2] for i in range(3)]


def doubled(whole):
    return jnp.concatenate([whole, whole], axis=0)


def join_pair(mine, other, lines, message, cot_pair):
    n = mine.shape[1]
    rows = mine.shape[0] - n - PAD
    late = lax.rem(lax.axis_index("tok"), 2) == 1
    a, b = mine[n + PAD :, :], other[n + PAD :, :]
    cot_pair[:rows, :] = jnp.where(late, b, a)
    cot_pair[rows:, :] = jnp.where(late, a, b)
    a, b = mine[: n + PAD, :], other[: n + PAD, :]
    early_map, (early_shift, early_last, early_decay) = unpack(jnp.where(late, b, a))
    late_map, (late_shift, late_last, late_decay) = unpack(jnp.where(late, a, b))
    slope, push = tangent(early_last, late_decay, lines[0:1, :])
    first = jnp.broadcast_to(early_shift * slope + push, (8, n))
    crossed = jnp.concatenate([early_map.astype(f32) * slope, first], axis=0)
    whole = dot(beside(crossed), doubled(late_map))
    pack(message, whole[:n], [whole[n : n + 1] + late_shift, late_last, early_decay])


def expand(near, pairs, lines, starts, shifts, slopes, offsets, wide, states, features, slots):
    rows, n = slopes.shape
    steps = rows // BLOCKS
    tok = lax.axis_index("tok")
    late, place = lax.rem(tok, 2) == 1, lax.div(tok, 2)
    for k, pair in enumerate(pairs):
        at = jnp.bitwise_xor(place, k)
        slots[at] = pair[...]
    mix, init, own_decay, own_drive = [lines[i : i + 1, :] for i in range(4)]
    wide_now = wide[...]

    def enter(current, last, decay):
        slope, push = tangent(last, decay, mix)
        return current * slope + push

    def passed(carried, block, taken):
        whole, (shift, last, decay) = unpack(block)
        current = dot(beside(enter(*carried, decay)), doubled(whole)) + shift
        return jnp.where(taken, current, carried[0]), jnp.where(taken, last, carried[1])

    carried = jnp.broadcast_to(init, (PAD, n)), init
    for q in range(len(pairs) - 1):
        carried = passed(carried, slots[q], q < place)
    carried = passed(carried, near[: n + PAD, :], late)
    entering = enter(*carried, own_decay)
    split = beside(entering)
    line = lax.broadcasted_iota(jnp.int32, (BLOCKS, n), 0)
    state = shifts[...]
    for b in range(1, BLOCKS):
        got = dot(split, doubled(starts[(b - 1) * n : b * n, :]))
        state = state + jnp.where(line == b, got[:BLOCKS], 0.0)
    for step in range(steps):
        picked = pl.ds(step, BLOCKS, stride=steps)
        moving, offset = state * slopes[picked, :], offsets[picked, :]
        if step == 0:
            moving = jnp.where(line == 0, entering[:BLOCKS], moving)
            offset = jnp.where(line == 0, own_drive, offset)
        state = times(moving, wide_now) + offset
        states[picked, :] = state
    features[...] = states[...].astype(bf16)


def stack(pieces, outs):
    rows = pieces[0].shape[0]
    place = lax.div(lax.axis_index("tok"), 2)
    for k, piece in enumerate(pieces):
        at = pl.ds(pl.multiple_of(jnp.bitwise_xor(place, k) * rows, rows), rows)
        for out in outs:
            out[at, :] = piece[...]


def activate(pre, grad):
    gate = 0.5 + 0.5 * jnp.tanh(0.5 * pre)
    hidden = (pre * gate).astype(bf16)
    return hidden, (grad * gate * (1.0 + pre * (1.0 - gate))).astype(bf16)


def lay(pieces, rows, side, out):
    tok, head = lax.axis_index("tok"), lax.axis_index("head")
    half, place = lax.rem(tok, 2), lax.div(tok, 2)
    places = range(out.shape[0] // rows)
    for d, (piece, first) in enumerate(pieces):
        n = piece.shape[1]
        lanes = pl.ds(pl.multiple_of(jnp.bitwise_xor(head, d) * n, n), n)
        whole = first is None
        for q in places:
            at = q if len(places) > 1 else place
            if whole:
                at = pl.ds(pl.multiple_of((2 * at + jnp.bitwise_xor(half, side)) * rows, rows), rows)
            else:
                at = pl.ds(pl.multiple_of(first + at * rows, rows), rows)
            out[q * rows : (q + 1) * rows, lanes] = piece[at, :]


def own_tokens(features, cots, w_up, w_down, outs, x, c):
    head = lax.axis_index("head")
    rows, n = x.shape[0], features[0][0].shape[1]
    lay(features, rows, 0, x)
    lay(cots, rows, 0, c)
    hidden, pre_grad = activate(dot(x[...], w_up[...]), dot(c[...], w_down[...]))
    out = dot(hidden, w_down[...], ((1,), (1,)))
    back = dot(pre_grad, w_up[...], ((1,), (1,)))
    group = lax.div(head, 2)
    groups = x.shape[1] // (2 * n)
    for at in range(groups):
        columns = slice(2 * n * at, 2 * n * (at + 1))
        both = jnp.concatenate([out[:, columns], back[:, columns]], axis=0).astype(bf16)
        for d in range(groups):

            @pl.when(jnp.bitwise_xor(group, d) == at)
            def _():
                outs[d][...] = both


def part_of(block, first, share):
    part = block[:share]
    for at in range(share, block.shape[0], share):
        part = jnp.where(first == at, block[at : at + share], part)
    return part


def gradients(features, cots, rows, side, w_up, w_down, before, outs, x, c):
    tok = lax.axis_index("tok")
    share, columns = outs[0].shape
    lay(features, rows, side, x)
    lay(cots, rows, side, c)
    block = max(share, 128)
    base = lax.div(tok * share, block)
    inner = tok * share - base * block
    lanes = pl.ds(pl.multiple_of(base * block, block), block)
    x_side, c_side = x[:, lanes].T, c[:, lanes].T
    chunk = 256

    def inner_products(first):
        at = slice(first, first + chunk)
        return dot(x[...], w_up[:, at]), dot(c[...], w_down[:, at])

    ahead = inner_products(0)
    for first in range(0, columns, chunk):
        now, at = ahead, slice(first, first + chunk)
        if first + chunk < columns:
            ahead = inner_products(first + chunk)
        hidden, pre_grad = activate(*now)
        totals = dot(x_side, pre_grad), dot(c_side, hidden)
        for out, total, old in zip(outs, totals, before or (None, None)):
            total = part_of(total, inner, share)
            out[:, at] = total if old is None else total + old[:, at]


def fold(keep, arrived, near, away):
    n = near.shape[1]
    total = keep[...].astype(f32)
    for part in arrived:
        total = total + part[...].astype(f32)
    odd = lax.rem(lax.axis_index("head"), 2) == 1
    near[...] = jnp.where(odd, total[:, n:], total[:, :n])
    away[...] = jnp.where(odd, total[:, :n], total[:, n:]).astype(bf16)


def finish(near, arrived, out, back):
    rows = out.shape[0]
    total = near[...] + arrived[...].astype(f32)
    out[...] = total[:rows].astype(bf16)
    back[...] = total[rows:].astype(bf16)


def call(body, outs, *operands, far=(), scratch=(), limit=16 * MIB, flops=10**6, moved=10**5):
    held = [pl.BlockSpec(memory_space=pltpu.HBM) for _ in far]
    return pl.pallas_call(
        body,
        out_shape=outs,
        in_specs=held + [VMEM] * len(operands),
        out_specs=jax.tree.map(lambda _: VMEM, outs),
        scratch_shapes=list(scratch),
        compiler_params=pltpu.CompilerParams(vmem_limit_bytes=limit),
        cost_estimate=pl.CostEstimate(flops=flops, bytes_accessed=moved, transcendentals=0),
    )(*far, *operands)


def swap(block, tok_bits, head_bits):
    toks, heads = lax.axis_size("tok"), lax.axis_size("head")
    route = [
        (t * heads + h, (t ^ tok_bits) * heads + (h ^ head_bits))
        for t in range(toks)
        for h in range(heads)
    ]
    return lax.ppermute(block, ("tok", "head"), route)


def on_device(guess, drive, decay, mixing, init_state, skew_gen, w_up, w_down, cotangent):
    rows, n = guess.shape
    toks, heads = lax.axis_size("tok"), lax.axis_size("head")
    places = toks // 2
    S, dma = jax.ShapeDtypeStruct, pltpu.SemaphoreType.DMA
    init, mix = init_state[None, :], mixing[None, :]
    wide = call(cayley, S((2 * n, 2 * n), bf16), skew_gen, flops=3 * 10**9)
    message, starts, shifts, slopes, offsets, lines = call(
        local_maps,
        (
            S((n + PAD + rows, n), bf16),
            S(((BLOCKS - 1) * n, n), bf16),
            S((BLOCKS, n), f32),
            S((rows, n), f32),
            S((rows, n), f32),
            S((8, n), f32),
        ),
        guess, decay, drive, mix, init, cotangent, wide, flops=3 * 10**9,
    )
    near = swap(message, 1, 0)
    pair, cot = call(
        join_pair, (S((n + PAD, n), bf16), S((2 * rows, n), bf16)),
        message, near, lines,
    )
    pairs = [pair] + [swap(pair, 2 * k, 0) for k in range(1, places)]
    cot_parts = [cot] + [swap(cot, 2 * k, 0) for k in range(1, places)]

    def expand_all(*refs):
        count = len(pairs)
        expand(refs[0], refs[1 : 1 + count], *refs[1 + count :])

    states, features = call(
        expand_all,
        (S((rows, n), f32), S((rows, n), bf16)),
        near, *pairs, lines, starts, shifts, slopes, offsets, wide,
        scratch=[pltpu.VMEM((places, n + PAD, n), bf16)], flops=3 * 10**9,
    )
    total = places * rows
    cots = {
        0: call(
            lambda *r: stack(r[1:-1], r[-1:]), S((toks * rows, n), bf16), features, *cot_parts
        )
    }
    parts = [features] + [swap(features, 2 * k, 0) for k in range(1, places)]
    for d in range(2, heads, 2):
        cots[d] = swap(cots[0], 0, d)
    lined = {0: call(lambda *r: stack(r[:-1], r[-1:]), S((total, n), bf16), *parts)}
    for d in range(2, heads, 2):
        lined[d] = swap(lined[0], 0, d)
    sides = [swap(lined[0], 1, d) for d in range(0, heads, 2)]
    for d in range(0, heads, 2):
        lined[d + 1] = swap(lined[d], 0, 1)
        cots[d + 1] = swap(cots[d], 0, 1)
    lined = [lined[d] for d in range(heads)]
    cots = [cots[d] for d in range(heads)]
    width = heads * n
    hidden_units = w_up.shape[1]
    limit = min(8 * MIB + 12 * total * width * 2, 56 * MIB)
    groups = heads // 2

    def parted(refs):
        features, cots = refs[:heads], refs[heads : 2 * heads]
        return [(ref, 0) for ref in features], [(ref, None) for ref in cots], refs[2 * heads :]

    def own(*refs):
        features, cots, refs = parted(refs)
        own_tokens(features, cots, refs[0], refs[1], refs[2 : 2 + groups], *refs[2 + groups :])

    keep, *far = call(
        own,
        tuple(S((2 * rows, 2 * n), bf16) for _ in range(groups)),
        *lined, *cots, w_up, w_down,
        scratch=[pltpu.VMEM((rows, width), bf16)] * 2, limit=limit,
        flops=10**9, moved=10**6,
    )
    arrived = [swap(far[d - 1], 0, 2 * d) for d in range(1, groups)]
    share = width // toks
    grads = (S((share, hidden_units), f32), S((share, hidden_units), f32))
    scratch = [pltpu.VMEM((total, width), bf16)] * 2

    def one(*refs):
        features, cots, refs = parted(refs)
        gradients(features, cots, rows, 0, refs[0], refs[1], None, refs[3:5], *refs[5:])

    half = call(
        one, grads, *lined, *cots, w_up, w_down, keep,
        scratch=scratch, limit=limit, flops=3 * 10**9, moved=4 * 10**6,
    )

    def line_up(*refs):
        for i, ref in enumerate(refs[1:-1]):
            refs[-1][i * total : (i + 1) * total, :] = ref[...]

    near_sides = call(line_up, S((groups * total, n), bf16), half[0], *sides)
    core_sides = swap(near_sides, 0, 1)

    def two(*refs):
        features = [(refs[d % 2], (d // 2) * total) for d in range(heads)]
        cots, refs = [(ref, None) for ref in refs[2 : 2 + heads]], refs[2 + heads :]
        gradients(features, cots, rows, 1, refs[0], refs[1], refs[2:4], refs[4:6], *refs[6:])

    grad_up, grad_down = call(
        two, grads, near_sides, core_sides, *cots, w_up, w_down, *half,
        scratch=scratch, limit=limit, flops=3 * 10**9, moved=4 * 10**6,
    )
    kept, away = call(
        lambda *r: fold(r[1], r[2:-2], *r[-2:]),
        (S((2 * rows, n), f32), S((2 * rows, n), bf16)),
        half[0], keep, *arrived, flops=4 * 10**9,
    )
    mlp_out, state_grad = call(
        finish, (S((rows, n), bf16), S((rows, n), bf16)), kept, swap(away, 0, 1), flops=4 * 10**9
    )
    return (states, mlp_out, state_grad, grad_up, grad_down)


def solution(mesh):
    placed = (
        P("tok", "head"),
        P("tok", "head"),
        P("tok", "head"),
        P("head"),
        P("head"),
        P("head", None, None),
        P(None, "head"),
        P(None, "head"),
        P("tok", "head"),
    )
    return jax.shard_map(
        on_device,
        mesh=mesh,
        in_specs=placed,
        out_specs=(P("tok", "head"),) * 5,
        check_vma=False,
    )
```

```python
import functools

import jax
import jax.numpy as jnp
from jax import lax
from jax.experimental import pallas as pl
from jax.experimental.pallas import tpu as pltpu
from jax.sharding import PartitionSpec as P

BLOCKS = 16
PAD = 16
MIB = 1 << 20
bf16, f32 = jnp.bfloat16, jnp.float32
exact_precision = lax.Precision.HIGHEST
VMEM = pl.BlockSpec(memory_space=pltpu.VMEM)


def dot(a, b, dims=((1,), (0,)), precision=None):
    return lax.dot_general(a, b, (dims, ((), ())), precision=precision, preferred_element_type=f32)


def halves(x):
    high = x.astype(bf16)
    return high, (x - high.astype(f32)).astype(bf16)


def beside(x):
    return jnp.concatenate(halves(x), axis=1)


def stationary(w):
    high, low = halves(w)
    top = jnp.concatenate([high, low], axis=1)
    bottom = jnp.concatenate([high, jnp.zeros_like(low)], axis=1)
    return jnp.concatenate([top, bottom], axis=0)


def times(x, wide):
    n = x.shape[1]
    both = dot(beside(x), wide)
    return both[:, :n] + both[:, n:]


def unit(n):
    return (
        lax.broadcasted_iota(jnp.int32, (n, n), 0) == lax.broadcasted_iota(jnp.int32, (n, n), 1)
    ).astype(f32)


def turned(skew):
    n = skew.shape[0]
    eye = unit(n)
    gram = eye - times(skew, stationary(skew))
    bound = jnp.max(jnp.sum(jnp.abs(gram), axis=0, keepdims=True))
    scale = 2.0 / (1.0 + bound)
    rest = eye - scale * gram

    def going(carried):
        return jnp.logical_and(carried[2] > 1e-4, carried[3] < 40)

    def lap(carried):
        power, inverse, size, count = carried
        both = times(jnp.concatenate([power, inverse], axis=0), stationary(power))
        return both[:n], inverse + both[n:], size * size, count + 1

    size = (bound - 1.0) / (bound + 1.0)
    _, inverse, _, _ = lax.while_loop(going, lap, (rest, eye, size, jnp.int32(0)))
    near = times(eye - skew, stationary(scale * inverse))
    miss = eye - dot(eye + skew, near, precision=exact_precision)
    near = near + times(near, stationary(miss))
    return 2.0 * near - eye


def fetch(pairs, sems):
    copies = [pltpu.make_async_copy(a, b, sems.at[i]) for i, (a, b) in enumerate(pairs)]
    for copy in copies:
        copy.start()
    return copies


def cayley(skew, wide):
    wide[...] = stationary(turned(skew[0]))


def tangent(before, decay, mix):
    bent = jnp.tanh(before)
    curve = 1.0 - bent * bent
    return (1.0 - mix) * decay + mix * curve, mix * (bent - curve * before)


def local_maps(
    guess, decay, drive, mixing, init, cot, wide,
    message, starts, shifts, slopes, offsets, lines,
):
    rows, n = guess.shape
    steps = rows // BLOCKS
    message[n + PAD :, :] = cot[...]
    wide_now = wide[...]
    slope, push = tangent(pltpu.roll(guess[...], 1, 0), decay[...], mixing[...])
    slopes[...] = slope
    offsets[...] = times(push, wide_now) + drive[...]
    own = [mixing[...], init[...], decay[0:1, :], drive[0:1, :]]
    lines[...] = jnp.concatenate(own + [jnp.zeros((4, n), f32)], axis=0)

    eye = unit(n)
    turn = wide_now[:n, :n].astype(f32) + wide_now[:n, n:].astype(f32)
    state = jnp.concatenate([eye] * BLOCKS + [jnp.zeros((BLOCKS, n), f32)], axis=0)
    line = lax.broadcasted_iota(jnp.int32, (BLOCKS, n), 0)
    for step in range(steps):
        slope = slopes[pl.ds(step, BLOCKS, stride=steps), :]
        spread = jnp.broadcast_to(slope[:, None, :], (BLOCKS, n, n)).reshape(BLOCKS * n, n)
        state = times(state * jnp.concatenate([spread, slope], axis=0), wide_now)
        shift = state[BLOCKS * n :] + offsets[pl.ds(step, BLOCKS, stride=steps), :]
        if step == 0:
            shift = jnp.where(line == 0, drive[0:1, :], shift)
            state = jnp.concatenate([turn, state[n : BLOCKS * n], shift], axis=0)
        else:
            state = jnp.concatenate([state[: BLOCKS * n], shift], axis=0)
    shift = state[BLOCKS * n :]
    maps = [
        jnp.concatenate(
            [state[b * n : (b + 1) * n], jnp.broadcast_to(shift[b : b + 1], (8, n))], axis=0
        )
        for b in range(BLOCKS)
    ]
    tail = lax.broadcasted_iota(jnp.int32, (n + 8, n), 0) >= n
    reach = 1
    while reach < BLOCKS:
        joined = list(maps)
        for base in range(reach, BLOCKS, 2 * reach):
            for b in range(base, base + reach):
                moved = times(maps[base - 1], stationary(maps[b][:n]))
                last = jnp.broadcast_to(maps[b][n : n + 1], (n + 8, n))
                joined[b] = moved + jnp.where(tail, last, 0.0)
        maps = joined
        reach *= 2
    shifts[0:1, :] = jnp.zeros((1, n), f32)
    for b in range(BLOCKS - 1):
        starts[b * n : (b + 1) * n, :] = maps[b][:n].astype(bf16)
        shifts[b + 1 : b + 2, :] = maps[b][n : n + 1]
    pack(message, maps[-1][:n], [maps[-1][n : n + 1], guess[rows - 1 :, :], decay[0:1, :]])


def pack(message, whole, lines):
    n = whole.shape[1]
    message[:n, :] = whole.astype(bf16)
    parts = [part.astype(f32) for row in lines for part in halves(row)]
    parts.append(jnp.zeros((PAD - len(parts), n), f32))
    message[n : n + PAD, :] = jnp.concatenate(parts, axis=0).astype(bf16)


def unpack(block):
    n = block.shape[1]
    lines = block[n : n + PAD].astype(f32)
    return block[:n], [lines[2 * i : 2 * i + 1] + lines[2 * i + 1 : 2 * i + 2] for i in range(3)]


def doubled(whole):
    return jnp.concatenate([whole, whole], axis=0)


def join_pair(mine, other, lines, message, cot_pair):
    n = mine.shape[1]
    rows = mine.shape[0] - n - PAD
    late = lax.rem(lax.axis_index("tok"), 2) == 1
    a, b = mine[n + PAD :, :], other[n + PAD :, :]
    cot_pair[:rows, :] = jnp.where(late, b, a)
    cot_pair[rows:, :] = jnp.where(late, a, b)
    a, b = mine[: n + PAD, :], other[: n + PAD, :]
    early_map, (early_shift, early_last, early_decay) = unpack(jnp.where(late, b, a))
    late_map, (late_shift, late_last, late_decay) = unpack(jnp.where(late, a, b))
    slope, push = tangent(early_last, late_decay, lines[0:1, :])
    first = jnp.broadcast_to(early_shift * slope + push, (8, n))
    crossed = jnp.concatenate([early_map.astype(f32) * slope, first], axis=0)
    whole = dot(beside(crossed), doubled(late_map))
    pack(message, whole[:n], [whole[n : n + 1] + late_shift, late_last, early_decay])


def expand(near, pairs, lines, starts, shifts, slopes, offsets, wide, states, features, slots):
    rows, n = slopes.shape
    steps = rows // BLOCKS
    tok = lax.axis_index("tok")
    late, place = lax.rem(tok, 2) == 1, lax.div(tok, 2)
    for k, pair in enumerate(pairs):
        at = jnp.bitwise_xor(place, k)
        slots[at] = pair[...]
    mix, init, own_decay, own_drive = [lines[i : i + 1, :] for i in range(4)]
    wide_now = wide[...]

    def enter(current, last, decay):
        slope, push = tangent(last, decay, mix)
        return current * slope + push

    def passed(carried, block, taken):
        whole, (shift, last, decay) = unpack(block)
        current = dot(beside(enter(*carried, decay)), doubled(whole)) + shift
        return jnp.where(taken, current, carried[0]), jnp.where(taken, last, carried[1])

    carried = jnp.broadcast_to(init, (PAD, n)), init
    for q in range(len(pairs) - 1):
        carried = passed(carried, slots[q], q < place)
    carried = passed(carried, near[: n + PAD, :], late)
    entering = enter(*carried, own_decay)
    split = beside(entering)
    line = lax.broadcasted_iota(jnp.int32, (BLOCKS, n), 0)
    state = shifts[...]
    for b in range(1, BLOCKS):
        got = dot(split, doubled(starts[(b - 1) * n : b * n, :]))
        state = state + jnp.where(line == b, got[:BLOCKS], 0.0)
    for step in range(steps):
        picked = pl.ds(step, BLOCKS, stride=steps)
        moving, offset = state * slopes[picked, :], offsets[picked, :]
        if step == 0:
            moving = jnp.where(line == 0, entering[:BLOCKS], moving)
            offset = jnp.where(line == 0, own_drive, offset)
        state = times(moving, wide_now) + offset
        states[picked, :] = state
    features[...] = states[...].astype(bf16)


def stack(pieces, outs):
    rows = pieces[0].shape[0]
    place = lax.div(lax.axis_index("tok"), 2)
    for k, piece in enumerate(pieces):
        at = pl.ds(pl.multiple_of(jnp.bitwise_xor(place, k) * rows, rows), rows)
        for out in outs:
            out[at, :] = piece[...]


def activate(pre, grad):
    gate = 0.5 + 0.5 * jnp.tanh(0.5 * pre)
    hidden = (pre * gate).astype(bf16)
    return hidden, (grad * gate * (1.0 + pre * (1.0 - gate))).astype(bf16)


def lay(pieces, rows, side, out):
    tok, head = lax.axis_index("tok"), lax.axis_index("head")
    half, place = lax.rem(tok, 2), lax.div(tok, 2)
    places = range(out.shape[0] // rows)
    for d, (piece, first) in enumerate(pieces):
        n = piece.shape[1]
        lanes = pl.ds(pl.multiple_of(jnp.bitwise_xor(head, d) * n, n), n)
        whole = first is None
        for q in places:
            at = q if len(places) > 1 else place
            if whole:
                at = pl.ds(pl.multiple_of((2 * at + jnp.bitwise_xor(half, side)) * rows, rows), rows)
            else:
                at = pl.ds(pl.multiple_of(first + at * rows, rows), rows)
            out[q * rows : (q + 1) * rows, lanes] = piece[at, :]


def own_tokens(features, cots, w_up, w_down, outs, x, c):
    head = lax.axis_index("head")
    rows, n = x.shape[0], features[0][0].shape[1]
    lay(features, rows, 0, x)
    lay(cots, rows, 0, c)
    hidden, pre_grad = activate(dot(x[...], w_up[...]), dot(c[...], w_down[...]))
    out = dot(hidden, w_down[...], ((1,), (1,)))
    back = dot(pre_grad, w_up[...], ((1,), (1,)))
    group = lax.div(head, 2)
    groups = x.shape[1] // (2 * n)
    for at in range(groups):
        columns = slice(2 * n * at, 2 * n * (at + 1))
        both = jnp.concatenate([out[:, columns], back[:, columns]], axis=0).astype(bf16)
        for d in range(groups):

            @pl.when(jnp.bitwise_xor(group, d) == at)
            def _():
                outs[d][...] = both


def part_of(block, first, share):
    part = block[:share]
    for at in range(share, block.shape[0], share):
        part = jnp.where(first == at, block[at : at + share], part)
    return part


def gradients(features, cots, rows, side, w_up, w_down, before, outs, x, c):
    tok = lax.axis_index("tok")
    share, columns = outs[0].shape
    lay(features, rows, side, x)
    lay(cots, rows, side, c)
    block = max(share, 128)
    base = lax.div(tok * share, block)
    inner = tok * share - base * block
    lanes = pl.ds(pl.multiple_of(base * block, block), block)
    x_side, c_side = x[:, lanes].T, c[:, lanes].T
    chunk = 256

    def inner_products(first):
        at = slice(first, first + chunk)
        return dot(x[...], w_up[:, at]), dot(c[...], w_down[:, at])

    ahead = inner_products(0)
    for first in range(0, columns, chunk):
        now, at = ahead, slice(first, first + chunk)
        if first + chunk < columns:
            ahead = inner_products(first + chunk)
        hidden, pre_grad = activate(*now)
        totals = dot(x_side, pre_grad), dot(c_side, hidden)
        for out, total, old in zip(outs, totals, before or (None, None)):
            total = part_of(total, inner, share)
            out[:, at] = total if old is None else total + old[:, at]


def fold(keep, arrived, near, away):
    n = near.shape[1]
    total = keep[...].astype(f32)
    for part in arrived:
        total = total + part[...].astype(f32)
    odd = lax.rem(lax.axis_index("head"), 2) == 1
    near[...] = jnp.where(odd, total[:, n:], total[:, :n])
    away[...] = jnp.where(odd, total[:, :n], total[:, n:]).astype(bf16)


def finish(near, arrived, out, back):
    rows = out.shape[0]
    total = near[...] + arrived[...].astype(f32)
    out[...] = total[:rows].astype(bf16)
    back[...] = total[rows:].astype(bf16)


def call(body, outs, *operands, far=(), scratch=(), limit=16 * MIB, flops=10**6, moved=10**5):
    held = [pl.BlockSpec(memory_space=pltpu.HBM) for _ in far]
    return pl.pallas_call(
        body,
        out_shape=outs,
        in_specs=held + [VMEM] * len(operands),
        out_specs=jax.tree.map(lambda _: VMEM, outs),
        scratch_shapes=list(scratch),
        compiler_params=pltpu.CompilerParams(vmem_limit_bytes=limit),
        cost_estimate=pl.CostEstimate(flops=flops, bytes_accessed=moved, transcendentals=0),
    )(*far, *operands)


def swap(block, tok_bits, head_bits):
    toks, heads = lax.axis_size("tok"), lax.axis_size("head")
    route = [
        (t * heads + h, (t ^ tok_bits) * heads + (h ^ head_bits))
        for t in range(toks)
        for h in range(heads)
    ]
    return lax.ppermute(block, ("tok", "head"), route)


def on_device(guess, drive, decay, mixing, init_state, skew_gen, w_up, w_down, cotangent):
    rows, n = guess.shape
    toks, heads = lax.axis_size("tok"), lax.axis_size("head")
    places = toks // 2
    S, dma = jax.ShapeDtypeStruct, pltpu.SemaphoreType.DMA
    init, mix = init_state[None, :], mixing[None, :]
    wide = call(cayley, S((2 * n, 2 * n), bf16), skew_gen, flops=3 * 10**9)
    message, starts, shifts, slopes, offsets, lines = call(
        local_maps,
        (
            S((n + PAD + rows, n), bf16),
            S(((BLOCKS - 1) * n, n), bf16),
            S((BLOCKS, n), f32),
            S((rows, n), f32),
            S((rows, n), f32),
            S((8, n), f32),
        ),
        guess, decay, drive, mix, init, cotangent, wide, flops=3 * 10**9,
    )
    near = swap(message, 1, 0)
    pair, cot = call(
        join_pair, (S((n + PAD, n), bf16), S((2 * rows, n), bf16)),
        message, near, lines,
    )
    pairs = [pair] + [swap(pair, 2 * k, 0) for k in range(1, places)]
    cot_parts = [cot] + [swap(cot, 2 * k, 0) for k in range(1, places)]

    def expand_all(*refs):
        count = len(pairs)
        expand(refs[0], refs[1 : 1 + count], *refs[1 + count :])

    states, features = call(
        expand_all,
        (S((rows, n), f32), S((rows, n), bf16)),
        near, *pairs, lines, starts, shifts, slopes, offsets, wide,
        scratch=[pltpu.VMEM((places, n + PAD, n), bf16)], flops=3 * 10**9,
    )
    total = places * rows
    cots = {
        0: call(
            lambda *r: stack(r[1:-1], r[-1:]), S((toks * rows, n), bf16), features, *cot_parts
        )
    }
    parts = [features] + [swap(features, 2 * k, 0) for k in range(1, places)]
    for d in range(2, heads, 2):
        cots[d] = swap(cots[0], 0, d)
    lined = {0: call(lambda *r: stack(r[:-1], r[-1:]), S((total, n), bf16), *parts)}
    for d in range(2, heads, 2):
        lined[d] = swap(lined[0], 0, d)
    sides = [swap(lined[0], 1, d) for d in range(0, heads, 2)]
    for d in range(0, heads, 2):
        lined[d + 1] = swap(lined[d], 0, 1)
        cots[d + 1] = swap(cots[d], 0, 1)
    lined = [lined[d] for d in range(heads)]
    cots = [cots[d] for d in range(heads)]
    width = heads * n
    hidden_units = w_up.shape[1]
    limit = min(8 * MIB + 12 * total * width * 2, 56 * MIB)
    groups = heads // 2

    def parted(refs):
        features, cots = refs[:heads], refs[heads : 2 * heads]
        return [(ref, 0) for ref in features], [(ref, None) for ref in cots], refs[2 * heads :]

    def own(*refs):
        features, cots, refs = parted(refs)
        own_tokens(features, cots, refs[0], refs[1], refs[2 : 2 + groups], *refs[2 + groups :])

    keep, *far = call(
        own,
        tuple(S((2 * rows, 2 * n), bf16) for _ in range(groups)),
        *lined, *cots, w_up, w_down,
        scratch=[pltpu.VMEM((rows, width), bf16)] * 2, limit=limit,
        flops=10**9, moved=10**6,
    )
    arrived = [swap(far[d - 1], 0, 2 * d) for d in range(1, groups)]
    share = width // toks
    grads = (S((share, hidden_units), f32), S((share, hidden_units), f32))
    scratch = [pltpu.VMEM((total, width), bf16)] * 2

    def one(*refs):
        features, cots, refs = parted(refs)
        refs[6][...] = refs[3][...]
        gradients(features, cots, rows, 0, refs[0], refs[1], None, refs[4:6], *refs[7:])

    *half, states = call(
        one, (*grads, S((rows, n), f32)), *lined, *cots, w_up, w_down, keep, states,
        scratch=scratch, limit=limit, flops=3 * 10**9, moved=4 * 10**6,
    )

    def line_up(*refs):
        for i, ref in enumerate(refs[1:-1]):
            refs[-1][i * total : (i + 1) * total, :] = ref[...]

    kept, away = call(
        lambda *r: fold(r[1], r[2:-2], *r[-2:]),
        (S((2 * rows, n), f32), S((2 * rows, n), bf16)),
        half[0], keep, *arrived, flops=4 * 10**9,
    )
    away = swap(away, 0, 1)
    near_sides = call(line_up, S((groups * total, n), bf16), kept, *sides)
    core_sides = swap(near_sides, 0, 1)

    def two(*refs):
        features = [(refs[d % 2], (d // 2) * total) for d in range(heads)]
        cots, refs = [(ref, None) for ref in refs[2 : 2 + heads]], refs[2 + heads :]
        finish(refs[4], refs[5], refs[8], refs[9])
        gradients(features, cots, rows, 1, refs[0], refs[1], refs[2:4], refs[6:8], *refs[10:])

    grad_up, grad_down, mlp_out, state_grad = call(
        two, (*grads, S((rows, n), bf16), S((rows, n), bf16)),
        near_sides, core_sides, *cots, w_up, w_down, *half, kept, away,
        scratch=scratch, limit=limit, flops=3 * 10**9, moved=4 * 10**6,
    )
    return (states, mlp_out, state_grad, grad_up, grad_down)


def solution(mesh):
    placed = (
        P("tok", "head"),
        P("tok", "head"),
        P("tok", "head"),
        P("head"),
        P("head"),
        P("head", None, None),
        P(None, "head"),
        P(None, "head"),
        P("tok", "head"),
    )
    return jax.shard_map(
        on_device,
        mesh=mesh,
        in_specs=placed,
        out_specs=(P("tok", "head"),) * 5,
        check_vma=False,
    )
```

```python
import functools

import jax
import jax.numpy as jnp
from jax import lax
from jax.experimental import pallas as pl
from jax.experimental.pallas import tpu as pltpu
from jax.sharding import PartitionSpec as P

BLOCKS = 16
PAD = 16
MIB = 1 << 20
bf16, f32 = jnp.bfloat16, jnp.float32
exact_precision = lax.Precision.HIGHEST
VMEM = pl.BlockSpec(memory_space=pltpu.VMEM)


def dot(a, b, dims=((1,), (0,)), precision=None):
    return lax.dot_general(a, b, (dims, ((), ())), precision=precision, preferred_element_type=f32)


def halves(x):
    high = x.astype(bf16)
    return high, (x - high.astype(f32)).astype(bf16)


def beside(x):
    return jnp.concatenate(halves(x), axis=1)


def stationary(w):
    high, low = halves(w)
    top = jnp.concatenate([high, low], axis=1)
    bottom = jnp.concatenate([high, jnp.zeros_like(low)], axis=1)
    return jnp.concatenate([top, bottom], axis=0)


def times(x, wide):
    n = x.shape[1]
    both = dot(beside(x), wide)
    return both[:, :n] + both[:, n:]


def unit(n):
    return (
        lax.broadcasted_iota(jnp.int32, (n, n), 0) == lax.broadcasted_iota(jnp.int32, (n, n), 1)
    ).astype(f32)


def turned(skew):
    n = skew.shape[0]
    eye = unit(n)
    gram = eye - times(skew, stationary(skew))
    bound = jnp.max(jnp.sum(jnp.abs(gram), axis=0, keepdims=True))
    scale = 2.0 / (1.0 + bound)
    rest = eye - scale * gram

    def going(carried):
        return jnp.logical_and(carried[2] > 1e-4, carried[3] < 40)

    def lap(carried):
        power, inverse, size, count = carried
        both = times(jnp.concatenate([power, inverse], axis=0), stationary(power))
        return both[:n], inverse + both[n:], size * size, count + 1

    size = (bound - 1.0) / (bound + 1.0)
    _, inverse, _, _ = lax.while_loop(going, lap, (rest, eye, size, jnp.int32(0)))
    near = times(eye - skew, stationary(scale * inverse))
    miss = eye - dot(eye + skew, near, precision=exact_precision)
    near = near + times(near, stationary(miss))
    return 2.0 * near - eye


def fetch(pairs, sems):
    copies = [pltpu.make_async_copy(a, b, sems.at[i]) for i, (a, b) in enumerate(pairs)]
    for copy in copies:
        copy.start()
    return copies


def cayley(skew, wide):
    wide[...] = stationary(turned(skew[0]))


def tangent(before, decay, mix):
    bent = jnp.tanh(before)
    curve = 1.0 - bent * bent
    return (1.0 - mix) * decay + mix * curve, mix * (bent - curve * before)


def local_maps(
    guess, decay, drive, mixing, init, cot, wide,
    message, starts, shifts, slopes, offsets, lines,
):
    rows, n = guess.shape
    steps = rows // BLOCKS
    message[n + PAD :, :] = cot[...]
    wide_now = wide[...]
    slope, push = tangent(pltpu.roll(guess[...], 1, 0), decay[...], mixing[...])
    slopes[...] = slope
    offsets[...] = times(push, wide_now) + drive[...]
    own = [mixing[...], init[...], decay[0:1, :], drive[0:1, :]]
    lines[...] = jnp.concatenate(own + [jnp.zeros((4, n), f32)], axis=0)

    eye = unit(n)
    turn = wide_now[:n, :n].astype(f32) + wide_now[:n, n:].astype(f32)
    state = jnp.concatenate([eye] * BLOCKS + [jnp.zeros((BLOCKS, n), f32)], axis=0)
    line = lax.broadcasted_iota(jnp.int32, (BLOCKS, n), 0)
    for step in range(steps):
        slope = slopes[pl.ds(step, BLOCKS, stride=steps), :]
        spread = jnp.broadcast_to(slope[:, None, :], (BLOCKS, n, n)).reshape(BLOCKS * n, n)
        state = times(state * jnp.concatenate([spread, slope], axis=0), wide_now)
        shift = state[BLOCKS * n :] + offsets[pl.ds(step, BLOCKS, stride=steps), :]
        if step == 0:
            shift = jnp.where(line == 0, drive[0:1, :], shift)
            state = jnp.concatenate([turn, state[n : BLOCKS * n], shift], axis=0)
        else:
            state = jnp.concatenate([state[: BLOCKS * n], shift], axis=0)
    shift = state[BLOCKS * n :]
    maps = [
        jnp.concatenate(
            [state[b * n : (b + 1) * n], jnp.broadcast_to(shift[b : b + 1], (8, n))], axis=0
        )
        for b in range(BLOCKS)
    ]
    tail = lax.broadcasted_iota(jnp.int32, (n + 8, n), 0) >= n
    reach = 1
    while reach < BLOCKS:
        joined = list(maps)
        for base in range(reach, BLOCKS, 2 * reach):
            for b in range(base, base + reach):
                moved = times(maps[base - 1], stationary(maps[b][:n]))
                last = jnp.broadcast_to(maps[b][n : n + 1], (n + 8, n))
                joined[b] = moved + jnp.where(tail, last, 0.0)
        maps = joined
        reach *= 2
    shifts[0:1, :] = jnp.zeros((1, n), f32)
    for b in range(BLOCKS - 1):
        starts[b * n : (b + 1) * n, :] = maps[b][:n].astype(bf16)
        shifts[b + 1 : b + 2, :] = maps[b][n : n + 1]
    pack(message, maps[-1][:n], [maps[-1][n : n + 1], guess[rows - 1 :, :], decay[0:1, :]])


def pack(message, whole, lines):
    n = whole.shape[1]
    message[:n, :] = whole.astype(bf16)
    parts = [part.astype(f32) for row in lines for part in halves(row)]
    parts.append(jnp.zeros((PAD - len(parts), n), f32))
    message[n : n + PAD, :] = jnp.concatenate(parts, axis=0).astype(bf16)


def unpack(block):
    n = block.shape[1]
    lines = block[n : n + PAD].astype(f32)
    return block[:n], [lines[2 * i : 2 * i + 1] + lines[2 * i + 1 : 2 * i + 2] for i in range(3)]


def doubled(whole):
    return jnp.concatenate([whole, whole], axis=0)


def join_pair(mine, other, lines, message, cot_pair):
    n = mine.shape[1]
    rows = mine.shape[0] - n - PAD
    late = lax.rem(lax.axis_index("tok"), 2) == 1
    a, b = mine[n + PAD :, :], other[n + PAD :, :]
    cot_pair[:rows, :] = jnp.where(late, b, a)
    cot_pair[rows:, :] = jnp.where(late, a, b)
    a, b = mine[: n + PAD, :], other[: n + PAD, :]
    early_map, (early_shift, early_last, early_decay) = unpack(jnp.where(late, b, a))
    late_map, (late_shift, late_last, late_decay) = unpack(jnp.where(late, a, b))
    slope, push = tangent(early_last, late_decay, lines[0:1, :])
    first = jnp.broadcast_to(early_shift * slope + push, (8, n))
    crossed = jnp.concatenate([early_map.astype(f32) * slope, first], axis=0)
    whole = dot(beside(crossed), doubled(late_map))
    pack(message, whole[:n], [whole[n : n + 1] + late_shift, late_last, early_decay])


def expand(near, pairs, lines, starts, shifts, slopes, offsets, wide, states, features, slots):
    rows, n = slopes.shape
    steps = rows // BLOCKS
    tok = lax.axis_index("tok")
    late, place = lax.rem(tok, 2) == 1, lax.div(tok, 2)
    for k, pair in enumerate(pairs):
        at = jnp.bitwise_xor(place, k)
        slots[at] = pair[...]
    mix, init, own_decay, own_drive = [lines[i : i + 1, :] for i in range(4)]
    wide_now = wide[...]

    def enter(current, last, decay):
        slope, push = tangent(last, decay, mix)
        return current * slope + push

    def passed(carried, block, taken):
        whole, (shift, last, decay) = unpack(block)
        current = dot(beside(enter(*carried, decay)), doubled(whole)) + shift
        return jnp.where(taken, current, carried[0]), jnp.where(taken, last, carried[1])

    carried = jnp.broadcast_to(init, (PAD, n)), init
    for q in range(len(pairs) - 1):
        carried = passed(carried, slots[q], q < place)
    carried = passed(carried, near[: n + PAD, :], late)
    entering = enter(*carried, own_decay)
    split = beside(entering)
    line = lax.broadcasted_iota(jnp.int32, (BLOCKS, n), 0)
    state = shifts[...]
    for b in range(1, BLOCKS):
        got = dot(split, doubled(starts[(b - 1) * n : b * n, :]))
        state = state + jnp.where(line == b, got[:BLOCKS], 0.0)
    for step in range(steps):
        picked = pl.ds(step, BLOCKS, stride=steps)
        moving, offset = state * slopes[picked, :], offsets[picked, :]
        if step == 0:
            moving = jnp.where(line == 0, entering[:BLOCKS], moving)
            offset = jnp.where(line == 0, own_drive, offset)
        state = times(moving, wide_now) + offset
        states[picked, :] = state
    features[...] = states[...].astype(bf16)


def stack(pieces, outs):
    rows = pieces[0].shape[0]
    place = lax.div(lax.axis_index("tok"), 2)
    for k, piece in enumerate(pieces):
        at = pl.ds(pl.multiple_of(jnp.bitwise_xor(place, k) * rows, rows), rows)
        for out in outs:
            out[at, :] = piece[...]


def activate(pre, grad):
    gate = 0.5 + 0.5 * jnp.tanh(0.5 * pre)
    hidden = (pre * gate).astype(bf16)
    return hidden, (grad * gate * (1.0 + pre * (1.0 - gate))).astype(bf16)


def lay(pieces, rows, side, out):
    tok, head = lax.axis_index("tok"), lax.axis_index("head")
    half, place = lax.rem(tok, 2), lax.div(tok, 2)
    places = range(out.shape[0] // rows)
    for d, (piece, first) in enumerate(pieces):
        n = piece.shape[1]
        lanes = pl.ds(pl.multiple_of(jnp.bitwise_xor(head, d) * n, n), n)
        whole = first is None
        for q in places:
            at = q if len(places) > 1 else place
            if whole:
                at = pl.ds(pl.multiple_of((2 * at + jnp.bitwise_xor(half, side)) * rows, rows), rows)
            else:
                at = pl.ds(pl.multiple_of(first + at * rows, rows), rows)
            out[q * rows : (q + 1) * rows, lanes] = piece[at, :]


def own_tokens(features, cots, w_up, w_down, outs, x, c):
    head = lax.axis_index("head")
    rows, n = x.shape[0], features[0][0].shape[1]
    lay(features, rows, 0, x)
    lay(cots, rows, 0, c)
    hidden, pre_grad = activate(dot(x[...], w_up[...]), dot(c[...], w_down[...]))
    out = dot(hidden, w_down[...], ((1,), (1,)))
    back = dot(pre_grad, w_up[...], ((1,), (1,)))
    group = lax.div(head, 2)
    groups = x.shape[1] // (2 * n)
    for at in range(groups):
        columns = slice(2 * n * at, 2 * n * (at + 1))
        both = jnp.concatenate([out[:, columns], back[:, columns]], axis=0).astype(bf16)
        for d in range(groups):

            @pl.when(jnp.bitwise_xor(group, d) == at)
            def _():
                outs[d][...] = both


def part_of(block, first, share):
    part = block[:share]
    for at in range(share, block.shape[0], share):
        part = jnp.where(first == at, block[at : at + share], part)
    return part


def gradients(features, cots, rows, side, w_up, w_down, before, outs, x, c):
    tok = lax.axis_index("tok")
    share, columns = outs[0].shape
    lay(features, rows, side, x)
    lay(cots, rows, side, c)
    block = max(share, 128)
    base = lax.div(tok * share, block)
    inner = tok * share - base * block
    lanes = pl.ds(pl.multiple_of(base * block, block), block)
    x_side, c_side = x[:, lanes].T, c[:, lanes].T
    chunk = 256

    def inner_products(first):
        at = slice(first, first + chunk)
        return dot(x[...], w_up[:, at]), dot(c[...], w_down[:, at])

    ahead = inner_products(0)
    for first in range(0, columns, chunk):
        now, at = ahead, slice(first, first + chunk)
        if first + chunk < columns:
            ahead = inner_products(first + chunk)
        hidden, pre_grad = activate(*now)
        totals = dot(x_side, pre_grad), dot(c_side, hidden)
        for out, total, old in zip(outs, totals, before or (None, None)):
            total = part_of(total, inner, share)
            out[:, at] = total if old is None else total + old[:, at]


def fold(keep, arrived, near, away):
    n = near.shape[1]
    total = keep[...].astype(f32)
    for part in arrived:
        total = total + part[...].astype(f32)
    odd = lax.rem(lax.axis_index("head"), 2) == 1
    near[...] = jnp.where(odd, total[:, n:], total[:, :n])
    away[...] = jnp.where(odd, total[:, :n], total[:, n:]).astype(bf16)


def finish(near, arrived, out, back):
    rows = out.shape[0]
    total = near[...] + arrived[...].astype(f32)
    out[...] = total[:rows].astype(bf16)
    back[...] = total[rows:].astype(bf16)


def call(body, outs, *operands, far=(), scratch=(), limit=16 * MIB, flops=10**6, moved=10**5):
    held = [pl.BlockSpec(memory_space=pltpu.HBM) for _ in far]
    return pl.pallas_call(
        body,
        out_shape=outs,
        in_specs=held + [VMEM] * len(operands),
        out_specs=jax.tree.map(lambda _: VMEM, outs),
        scratch_shapes=list(scratch),
        compiler_params=pltpu.CompilerParams(vmem_limit_bytes=limit),
        cost_estimate=pl.CostEstimate(flops=flops, bytes_accessed=moved, transcendentals=0),
    )(*far, *operands)


def swap(block, tok_bits, head_bits):
    toks, heads = lax.axis_size("tok"), lax.axis_size("head")
    route = [
        (t * heads + h, (t ^ tok_bits) * heads + (h ^ head_bits))
        for t in range(toks)
        for h in range(heads)
    ]
    return lax.ppermute(block, ("tok", "head"), route)


def on_device(guess, drive, decay, mixing, init_state, skew_gen, w_up, w_down, cotangent):
    rows, n = guess.shape
    toks, heads = lax.axis_size("tok"), lax.axis_size("head")
    places = toks // 2
    S, dma = jax.ShapeDtypeStruct, pltpu.SemaphoreType.DMA
    init, mix = init_state[None, :], mixing[None, :]
    wide = call(cayley, S((2 * n, 2 * n), bf16), skew_gen, flops=3 * 10**9)
    message, starts, shifts, slopes, offsets, lines = call(
        local_maps,
        (
            S((n + PAD + rows, n), bf16),
            S(((BLOCKS - 1) * n, n), bf16),
            S((BLOCKS, n), f32),
            S((rows, n), f32),
            S((rows, n), f32),
            S((8, n), f32),
        ),
        guess, decay, drive, mix, init, cotangent, wide, flops=3 * 10**9,
    )
    near = swap(message, 1, 0)
    pair, cot = call(
        join_pair, (S((n + PAD, n), bf16), S((2 * rows, n), bf16)),
        message, near, lines,
    )
    pairs = [pair] + [swap(pair, 2 * k, 0) for k in range(1, places)]
    cot_parts = [cot] + [swap(cot, 2 * k, 0) for k in range(1, places)]

    def expand_all(*refs):
        count = len(pairs)
        expand(refs[0], refs[1 : 1 + count], *refs[1 + count :])

    states, features = call(
        expand_all,
        (S((rows, n), f32), S((rows, n), bf16)),
        near, *pairs, lines, starts, shifts, slopes, offsets, wide,
        scratch=[pltpu.VMEM((places, n + PAD, n), bf16)], flops=3 * 10**9,
    )
    total = places * rows
    cots = {
        0: call(
            lambda *r: stack(r[1:-1], r[-1:]), S((toks * rows, n), bf16), features, *cot_parts
        )
    }
    parts = [features] + [swap(features, 2 * k, 0) for k in range(1, places)]
    for d in range(2, heads, 2):
        cots[d] = swap(cots[0], 0, d)
    lined = {0: call(lambda *r: stack(r[:-1], r[-1:]), S((total, n), bf16), *parts)}
    for d in range(2, heads, 2):
        lined[d] = swap(lined[0], 0, d)
    sides = [swap(lined[0], 1, d) for d in range(0, heads, 2)]
    for d in range(0, heads, 2):
        lined[d + 1] = swap(lined[d], 0, 1)
        cots[d + 1] = swap(cots[d], 0, 1)
    lined = [lined[d] for d in range(heads)]
    cots = [cots[d] for d in range(heads)]
    width = heads * n
    hidden_units = w_up.shape[1]
    limit = min(8 * MIB + 12 * total * width * 2, 56 * MIB)
    groups = heads // 2

    def parted(refs):
        features, cots = refs[:heads], refs[heads : 2 * heads]
        return [(ref, 0) for ref in features], [(ref, None) for ref in cots], refs[2 * heads :]

    def own(*refs):
        features, cots, refs = parted(refs)
        own_tokens(features, cots, refs[0], refs[1], refs[2 : 2 + groups], *refs[2 + groups :])

    keep, *far = call(
        own,
        tuple(S((2 * rows, 2 * n), bf16) for _ in range(groups)),
        *lined, *cots, w_up, w_down,
        scratch=[pltpu.VMEM((rows, width), bf16)] * 2, limit=limit,
        flops=10**9, moved=10**6,
    )
    arrived = [swap(far[d - 1], 0, 2 * d) for d in range(1, groups)]
    share = width // toks
    grads = (S((share, hidden_units), f32), S((share, hidden_units), f32))
    scratch = [pltpu.VMEM((total, width), bf16)] * 2

    def one(*refs):
        features, cots, refs = parted(refs)
        refs[6][...] = refs[3][...]
        gradients(features, cots, rows, 0, refs[0], refs[1], None, refs[4:6], *refs[7:])

    *half, states = call(
        one, (*grads, S((rows, n), f32)), *lined, *cots, w_up, w_down, keep, states,
        scratch=scratch, limit=limit, flops=3 * 10**9, moved=4 * 10**6,
    )

    def line_up(*refs):
        for i, ref in enumerate(refs[1:-1]):
            refs[-1][i * total : (i + 1) * total, :] = ref[...]

    kept, away = call(
        lambda *r: fold(r[1], r[2:-2], *r[-2:]),
        (S((2 * rows, n), f32), S((2 * rows, n), bf16)),
        half[0], keep, *arrived, flops=4 * 10**9,
    )
    away = swap(away, 0, 1)
    near_sides = call(line_up, S((groups * total, n), bf16), half[0], *sides)
    core_sides = swap(near_sides, 0, 1)

    def two(*refs):
        features = [(refs[d % 2], (d // 2) * total) for d in range(heads)]
        cots, refs = [(ref, None) for ref in refs[2 : 2 + heads]], refs[2 + heads :]
        finish(refs[4], refs[5], refs[8], refs[9])
        gradients(features, cots, rows, 1, refs[0], refs[1], refs[2:4], refs[6:8], *refs[10:])

    grad_up, grad_down, mlp_out, state_grad = call(
        two, (*grads, S((rows, n), bf16), S((rows, n), bf16)),
        near_sides, core_sides, *cots, w_up, w_down, *half, kept, away,
        scratch=scratch, limit=limit, flops=3 * 10**9, moved=4 * 10**6,
    )
    return (states, mlp_out, state_grad, grad_up, grad_down)


def solution(mesh):
    placed = (
        P("tok", "head"),
        P("tok", "head"),
        P("tok", "head"),
        P("head"),
        P("head"),
        P("head", None, None),
        P(None, "head"),
        P(None, "head"),
        P("tok", "head"),
    )
    return jax.shard_map(
        on_device,
        mesh=mesh,
        in_specs=placed,
        out_specs=(P("tok", "head"),) * 5,
        check_vma=False,
    )
```
